128 devices in a mesh: rep: 32 (over z, y, x_lo), shard: 4 (over x_hi, core).
Axes of the slice: x: 4 (x_hi: 2, x_lo: 2; x = x_hi * 2 + x_lo), y: 4, z: 4, core: 2. Of those that a mesh axis runs over, the one named last changes fastest.
Arguments:
- inputs: bfloat16 [1536, 197, 384], P(('rep', 'shard')), may hold values from -6 to 6
- out_grad: bfloat16 [1536, 197, 384], P(('rep', 'shard')), may hold values from -6 to 6
- ln1_gain: bfloat16 [384], P('shard'), may hold values from 0.099609375 to 1.8984375
- ln1_shift: bfloat16 [384], P('shard'), may hold values from -3 to 3
- qkv_weight: bfloat16 [384, 1152], P('shard'), may hold values from -0.3125 to 0.3125
- qv_bias: bfloat16 [768], P('shard'), may hold values from -3 to 3
- out_weight: bfloat16 [384, 384], P('shard'), may hold values from -1.25 to 1.25
- out_bias: bfloat16 [384], P('shard'), may hold values from -3 to 3
- ln2_gain: bfloat16 [384], P('shard'), may hold values from 0.099609375 to 1.8984375
- ln2_shift: bfloat16 [384], P('shard'), may hold values from -3 to 3
- up_weight: bfloat16 [384, 1536], P('shard'), may hold values from -0.3125 to 0.3125
- up_bias: bfloat16 [1536], P('shard'), may hold values from -3 to 3
- down_weight: bfloat16 [1536, 384], P('shard'), may hold values from -0.15625 to 0.15625
- down_bias: bfloat16 [384], P('shard'), may hold values from -3 to 3
Outputs:
- outputs: bfloat16 [1536, 197, 384], P(('rep', 'shard'))
- input_grad: bfloat16 [1536, 197, 384], P(('rep', 'shard'))
- ln1_gain_grad: float32 [384], P('shard')
- ln1_shift_grad: float32 [384], P('shard')
- qkv_weight_grad: float32 [384, 1152], P('shard')
- qv_bias_grad: float32 [768], P('shard')
- out_weight_grad: float32 [384, 384], P('shard')
- out_bias_grad: float32 [384], P('shard')
- ln2_gain_grad: float32 [384], P('shard')
- ln2_shift_grad: float32 [384], P('shard')
- up_weight_grad: float32 [384, 1536], P('shard')
- up_bias_grad: float32 [1536], P('shard')
- down_weight_grad: float32 [1536, 384], P('shard')
- down_bias_grad: float32 [384], P('shard')
The draws below stay inside these ranges and needn't reach their ends.
All inputs are finite; a program needn't handle non-finite values.
Results may differ from the reference program's by a relative error of at most 0.029.
Values may be sent and summed in bfloat16 or wider, within the bound.
A program may use at most 256 MiB of HBM per device.

```python
import jax
import jax.numpy as jnp
from jax import lax

D = 384
HEADS = 6
HEAD_DIM = 64
FF = 1536
SEQ = 197
IMAGES = 1536


def level_of(rng, shape, shards, least, top_value):
    factor_of = 1.0
    for axis_at, blocks in shards:
        heights = jax.random.uniform(jax.random.fold_in(jax.random.fold_in(rng, 6), axis_at), (blocks,), jnp.float32, least / len(shards), top_value / len(shards))
        factor_of = factor_of * jnp.repeat(jnp.exp(heights), shape[axis_at] // blocks).reshape((-1,) + (1,) * (len(shape) - 1 - axis_at))
    return factor_of


def noise(rng, dims, spread, limit, shards=(), kind=jnp.bfloat16):
    values = spread * jax.random.normal(rng, dims, jnp.float32)
    if shards:
        values = values * level_of(rng, dims, shards, -0.22, 0.18)
    return jnp.clip(values, -limit, limit).astype(kind)


def setup_inputs(seed: int = 0) -> dict:
    key_list = jax.random.split(jax.random.key(seed), 15)
    return {
        "inputs": noise(key_list[0], (IMAGES, SEQ, D), 1.0, 6.0, ((0, 128),)),
        "out_grad": noise(key_list[1], (IMAGES, SEQ, D), 1.0, 6.0, ((0, 128),)),
        "ln1_gain": jnp.clip(1.0 + 0.18 * jax.random.normal(key_list[2], (D,), jnp.float32), 0.099609375, 1.8984375).astype(jnp.bfloat16),
        "ln1_shift": noise(key_list[3], (D,), 0.3, 3.0, ((0, 4),)),
        "qkv_weight": noise(key_list[4], (D, 3 * D), D ** -0.5, 0.3125, ((0, 4),)),
        "qv_bias": noise(key_list[5], (2 * D,), 0.5, 3.0, ((0, 4),)),
        "out_weight": noise(key_list[6], (D, D), (D // 16) ** -0.5, 1.25, ((0, 4),)),
        "out_bias": noise(key_list[7], (D,), 0.3, 3.0, ((0, 4),)),
        "ln2_gain": jnp.clip(1.0 + 0.18 * jax.random.normal(key_list[8], (D,), jnp.float32), 0.099609375, 1.8984375).astype(jnp.bfloat16),
        "ln2_shift": noise(key_list[9], (D,), 0.3, 3.0, ((0, 4),)),
        "up_weight": noise(key_list[10], (D, FF), D ** -0.5, 0.3125, ((0, 4),)),
        "up_bias": noise(key_list[11], (FF,), 0.5, 3.0, ((0, 4),)),
        "down_weight": noise(key_list[12], (FF, D), FF ** -0.5, 0.15625, ((0, 4),)),
        "down_bias": noise(key_list[13], (D,), 0.3, 3.0, ((0, 4),)),
    }


@jax.custom_vjp
def low(v):
    return lax.optimization_barrier(v.astype(jnp.bfloat16)).astype(jnp.float32)

@jax.custom_vjp
def low_back(v):
    return v

def low_keep(v):
    return (low(v), None)

def low_pass(kept, grad):
    return (grad,)

def back_keep(v):
    return (v, None)

def back_low(kept, grad):
    return (low(grad),)
low.defvjp(low_keep, low_pass)
low_back.defvjp(back_keep, back_low)
highest = lax.Precision.HIGHEST
block_images = 16

def layer_norm(values, gain_vec, shift_vec):
    average = lax.optimization_barrier(jnp.mean(values, axis=-1, keepdims=True))
    centred = values - average
    variance = lax.optimization_barrier(jnp.mean(centred * centred, axis=-1, keepdims=True))
    return centred * lax.rsqrt(variance + 1e-06) * gain_vec + shift_vec

def forward(inputs, ln1_gain, ln1_shift, qkv_weight, qv_bias, out_weight, out_bias, ln2_gain, ln2_shift, up_weight, up_bias, down_weight, down_bias):
    images, length, width = inputs.shape
    score_scale = HEAD_DIM ** (-0.5)

    def heads_view(tensor):
        return tensor.reshape(images, length, HEADS, HEAD_DIM)
    normed = low(layer_norm(inputs, ln1_gain, ln1_shift))
    packed = jnp.einsum('bsd,de->bse', normed, qkv_weight, precision=highest)
    query = low_back(low(packed[..., :width] + qv_bias[:width]))
    key_rows = low_back(low(packed[..., width:2 * width]))
    value_rows = low_back(low(packed[..., 2 * width:] + qv_bias[width:]))
    scores = jnp.einsum('bqhe,bkhe->bhqk', heads_view(query), heads_view(key_rows), precision=highest) * score_scale
    scores = low_back(scores)
    shifted = scores - lax.optimization_barrier(jnp.max(scores, axis=-1, keepdims=True))
    expo = jnp.exp(shifted)
    probs = low(expo / lax.optimization_barrier(jnp.sum(expo, axis=-1, keepdims=True)))
    mixed = jnp.einsum('bhqk,bkhe->bqhe', probs, heads_view(value_rows), precision=highest)
    mixed = low_back(low(mixed.reshape(images, length, width)))
    branch = low_back(jnp.einsum('bsd,de->bse', mixed, out_weight, precision=highest) + out_bias)
    middle = inputs + branch
    normed_two = low(layer_norm(middle, ln2_gain, ln2_shift))
    hidden_pre = low_back(jnp.einsum('bsd,df->bsf', normed_two, up_weight, precision=highest) + up_bias)
    activated = low(jax.nn.gelu(hidden_pre, approximate=False))
    return middle + jnp.einsum('bsf,fd->bsd', activated, down_weight, precision=highest) + down_bias

def reference(inputs, out_grad, ln1_gain, ln1_shift, qkv_weight, qv_bias, out_weight, out_bias, ln2_gain, ln2_shift, up_weight, up_bias, down_weight, down_bias):
    params = tuple((member.astype(jnp.float32) for member in (ln1_gain, ln1_shift, qkv_weight, qv_bias, out_weight, out_bias, ln2_gain, ln2_shift, up_weight, up_bias, down_weight, down_bias)))
    block_count = IMAGES // block_images
    stacked_in = inputs.reshape(block_count, block_images, SEQ, D)
    stacked_cot = out_grad.reshape(block_count, block_images, SEQ, D)

    def scan_step(totals, pieces):
        block_in, block_cot = pieces
        result, pullback = jax.vjp(forward, block_in.astype(jnp.float32), *params)
        gradients = pullback(block_cot.astype(jnp.float32))
        summed = tuple((earlier + later for earlier, later in zip(totals, gradients[1:])))
        return (summed, (result.astype(jnp.bfloat16), gradients[0].astype(jnp.bfloat16)))
    initial = tuple((jnp.zeros_like(member) for member in params))
    totals, (outputs, input_grad) = lax.scan(scan_step, initial, (stacked_in, stacked_cot))
    return (outputs.reshape(IMAGES, SEQ, D), input_grad.reshape(IMAGES, SEQ, D), totals[0], totals[1], totals[2], totals[3], totals[4], totals[5], totals[6], totals[7], totals[8], totals[9], totals[10], totals[11])
```

```python
import math

import jax
import jax.numpy as jnp
from jax import lax
from jax.experimental import pallas as pl
from jax.experimental.pallas import tpu as pltpu
from jax.sharding import PartitionSpec as P

NI, SEQ, D, FF, HEADS = 12, 197, 384, 1536, 6
PAD = 208
ROWS = NI * PAD
TROWS = 2560
F32, BF16 = jnp.float32, jnp.bfloat16


def mm(a, b):
    return lax.dot_general(a, b, (((1,), (0,)), ((), ())), preferred_element_type=F32)


def mm_nt(a, b):
    return lax.dot_general(a, b, (((1,), (1,)), ((), ())), preferred_element_type=F32)


def mm_tn(a, b):
    return lax.dot_general(a, b, (((0,), (0,)), ((), ())), preferred_element_type=F32)


def norm_parts(v):
    avg = jnp.mean(v, axis=-1, keepdims=True)
    cen = v - avg
    var = jnp.mean(cen * cen, axis=-1, keepdims=True)
    rs = lax.rsqrt(var + 1e-6)
    return cen * rs, rs


def norm_back(e, n, rs):
    return rs * (e - jnp.mean(e, axis=-1, keepdims=True) - n * jnp.mean(e * n, axis=-1, keepdims=True))


def gelu_both(u):
    a = jnp.abs(u)
    d = 1.0 + (0.3275911 * math.sqrt(0.5)) * a
    t = 1.0 / d
    e = jnp.exp2(u * u * (-0.5 * math.log2(math.e)))
    p = (0.5 * 1.061405429) * t - (0.5 * 1.453152027)
    p = p * t + (0.5 * 1.421413741)
    p = p * t - (0.5 * 0.284496736)
    p = p * t + (0.5 * 0.254829592)
    tail = p * t * e
    phi = jnp.where(u < 0, tail, 1.0 - tail)
    return u * phi, phi + u * (e * (1.0 / math.sqrt(2 * math.pi)))


def colsum(v):
    return jnp.sum(v, axis=0, keepdims=True)

CH1, CH2, CH4 = 2, 2, 2
MESH = pl.DeviceIdType.MESH

UP_ROW, DOWN_ROW, OUT_ROW, QKV_ROW = 0, 1152, 2304, 2592
GROWS = 3584
GROUPS = ((0, 160), (2560, 32), (3072, 32))


class Comm:
    def __init__(self, ssem, rsem):
        self.ssem, self.rsem = ssem, rsem
        rep, shard = lax.axis_index("rep"), lax.axis_index("shard")
        self.z, self.y, self.lo = rep // 8, (rep // 2) % 4, rep % 2
        self.hi, self.core, self.plane = shard // 2, shard % 2, rep // 2
        self.sibling = (rep, self.hi * 2 + 1 - self.core)
        self.across = (self.plane * 2 + 1 - self.lo, (1 - self.hi) * 2 + self.core)
        self.row = []
        for dh, dl in ((0, 1), (1, 0), (1, 1)):
            ph, plo = (self.hi + dh) % 2, (self.lo + dl) % 2
            self.row.append(((self.plane * 2 + plo, ph * 2 + self.core), ph))
        self.planes = []
        for d in range(1, 16):
            pz, py = (self.z + d // 4) % 4, (self.y + d % 4) % 4
            q = pz * 4 + py
            self.planes.append(((q * 2 + self.lo, shard), q))

    def barrier(self):
        sem = pltpu.get_barrier_semaphore()
        peers = [self.sibling] + [d for d, _ in self.row] + [d for d, _ in self.planes]
        for dev in peers:
            pl.semaphore_signal(sem, inc=1, device_id=dev, device_id_type=MESH)
        pl.semaphore_wait(sem, len(peers))

    def copy(self, src, dst, slot, dev):
        return pltpu.make_async_remote_copy(
            src_ref=src, dst_ref=dst, send_sem=self.ssem.at[slot], recv_sem=self.rsem.at[slot],
            device_id=dev, device_id_type=MESH,
        )


class Reduce:
    def __init__(self, comm, base, grads, fin, start, n, rcore, rplane, part, rrow, scatter=True):
        c = comm
        self.c, self.n, self.scatter, self.start = c, n, scatter, start
        total = 16 * n if scatter else n
        self.grads, self.rcore, self.rplane, self.part, self.rrow, self.fin = (
            grads, rcore, rplane, part, rrow, fin)
        self.total = total
        rows = pl.ds(start, total)
        self.rows = rows
        self.core_copy = c.copy(grads.at[1 - c.core, :, rows, :], rcore, base, c.sibling)

        def piece(q):
            return pl.ds(pl.multiple_of(start + q * n, 16), n) if scatter else rows

        self.piece = piece
        self.plane_copies = [
            c.copy(grads.at[c.core, :, piece(q), :], rplane.at[d], base + 1 + d, dev)
            for d, (dev, q) in enumerate(c.planes)
        ]
        self.row_copies = [
            c.copy(part.at[h], rrow.at[d], base + 16 + d, dev)
            for d, (dev, h) in enumerate(c.row)
        ]
        if scatter:
            mine = piece(c.plane)
            self.back_copies = [
                c.copy(fin.at[mine, :], fin.at[mine, :], base + 19 + d, dev)
                for d, (dev, q) in enumerate(c.planes)
            ]

    def send_core(self):
        self.core_copy.start()

    def send_planes(self):
        self.core_copy.wait()
        step = 256 if self.total % 256 == 0 else 16

        @pl.loop(0, self.total // step)
        def _(b):
            off = pl.multiple_of(b * step, 16)
            r = pl.ds(pl.multiple_of(self.start + off, 16), step)
            for h in range(2):
                s = self.grads[self.c.core, h, r, :].astype(F32) + self.rcore[h, pl.ds(off, step), :].astype(F32)
                self.grads[self.c.core, h, r, :] = s.astype(BF16)

        for cp in self.plane_copies:
            cp.start()

    def send_row(self):
        for cp in self.plane_copies:
            cp.wait()
        for h in range(2):
            s = self.grads[self.c.core, h, self.piece(self.c.plane), :].astype(F32)
            for d in range(15):
                s = s + self.rplane[d, h].astype(F32)
            self.part[h] = s.astype(BF16)
        for cp in self.row_copies:
            cp.start()

    def send_back(self):
        for cp in self.row_copies:
            cp.wait()
        s = self.part[self.c.hi].astype(F32)
        for d in range(3):
            s = s + self.rrow[d].astype(F32)
        if self.scatter:
            self.fin[self.piece(self.c.plane), :] = s.astype(BF16)
            for cp in self.back_copies:
                cp.start()
        else:
            self.fin[...] = s.astype(BF16)

    def finish(self):
        for cp in self.back_copies:
            cp.wait()


def padded(ref, i, tmp):
    tmp[0:SEQ, :] = ref[i].astype(F32)
    return tmp[...]


def body(x_ref, dy_ref, vin_ref, wqkv_in, wo_in, wup_in, wd_in,
         out_ref, ig_ref, fin_ref, finv_ref,
         stage, out_sem, tmp, dys, dyT, tT, h1s, qkv, ps, cs, h2s, gs, dus, dbs,
         vecs_all, wqkv, wo, wup, wd, vec_ref, gvec, grads, gradv,
         rcore0, rplane0, part0, rrow0, rcore1, rplane1, part1, rrow1,
         rcore2, rplane2, part2, rrow2, rcorev, rplanev, partv, rrowv, fin, finv, ssem, rsem):
    dy_copy = pltpu.make_async_copy(dy_ref, stage, out_sem)
    dy_copy.start()
    comm = Comm(ssem, rsem)
    shard = comm.hi * 2 + comm.core
    theirs = (1 - comm.hi) * 2 + comm.core

    def place(full, s):
        n = full.shape[0] // 4
        return full.at[pl.ds(pl.multiple_of(s * n, 16), n)]

    params = ((wqkv_in, wqkv), (vin_ref, vecs_all), (wo_in, wo), (wup_in, wup), (wd_in, wd))
    for own, full in params:
        n = own.shape[0]
        full[pl.ds(pl.multiple_of(shard * n, 16), n), :] = own[...]
    comm.barrier()
    first, second, third = [], [], []
    for j, (own, full) in enumerate(params):
        first.append(comm.copy(own, place(full, shard), 3 * j, comm.across))
        second.append(comm.copy(own, place(full, shard), 3 * j + 1, comm.sibling))
        third.append(comm.copy(place(full, theirs), place(full, theirs), 3 * j + 2, comm.sibling))
        first[j].start()
        second[j].start()

    def forward(j):
        first[j].wait_recv()
        third[j].start()

    def gathered(j):
        second[j].wait_recv()
        third[j].wait_recv()

    red = [Reduce(comm, 16 + 40 * g, grads, fin, start, n, *bufs)
           for g, ((start, n), bufs) in enumerate(zip(GROUPS, (
               (rcore0, rplane0, part0, rrow0), (rcore1, rplane1, part1, rrow1),
               (rcore2, rplane2, part2, rrow2))))]
    redv = Reduce(comm, 136, gradv, finv, 0, 16, rcorev, rplanev, partv, rrowv, scatter=False)

    def vec(r):
        return vec_ref[r:r + 1, :]

    def vcat(r, n):
        return jnp.concatenate([vec_ref[r + j:r + j + 1, :] for j in range(n)], axis=1)

    tmp[...] = jnp.zeros_like(tmp)
    gvec[...] = jnp.zeros_like(gvec)
    for s in (dys, h1s, cs, h2s, gs, dus, dbs, qkv):
        s[ROWS:TROWS, :] = jnp.zeros((TROWS - ROWS, s.shape[1]), s.dtype)
    grads[:, :, QKV_ROW + 864:, :] = jnp.zeros((2, 2, GROWS - QKV_ROW - 864, 128), BF16)
    dy_copy.wait()

    @pl.loop(0, NI)
    def _(i):
        r = pl.ds(pl.multiple_of(i * PAD, 16), PAD)
        dy = padded(stage, i, tmp)
        dys[r, :] = dy.astype(BF16)
        gvec[5:6, :] += colsum(dy)

    forward(0)
    forward(1)
    gathered(1)
    vec_ref[...] = (
        vecs_all[0:16, :].astype(F32) + vecs_all[16:32, :].astype(F32)
        + vecs_all[32:48, :].astype(F32) + vecs_all[48:64, :].astype(F32)
    )

    @pl.loop(0, NI)
    def _(i):
        r = pl.ds(pl.multiple_of(i * PAD, 16), PAD)
        n, _ = norm_parts(padded(x_ref, i, tmp))
        h1s[r, :] = (n * vec(0) + vec(1)).astype(BF16)

    def transpose_into(dst, src):
        @pl.loop(0, TROWS // 256)
        def _(b):
            r = pl.ds(pl.multiple_of(b * 256, 256), 256)
            dst[:, r] = src[r, :].T

    transpose_into(dyT, dys)
    gathered(0)

    lane = lax.broadcasted_iota(jnp.int32, (1, 128), 1)
    halves = (lane < 64, lane >= 64)
    keycol = lax.broadcasted_iota(jnp.int32, (1, PAD), 1) < SEQ
    zero = jnp.zeros((), BF16)

    def half(v, h):
        return jnp.where(halves[h], v, zero)

    @pl.loop(0, NI // CH1)
    def _(c):
        r = pl.ds(pl.multiple_of(c * (CH1 * PAD), 16), CH1 * PAD)
        p = mm(h1s[r, :], wqkv[...]) + vcat(6, 3)
        qkv[r, 0:D] = (p[:, 0:D] * 0.125).astype(BF16)
        qkv[r, D:3 * D] = p[:, D:].astype(BF16)

    def attention(first_image, last_image):
        @pl.loop(first_image, last_image)
        def _(i):
            r = pl.ds(pl.multiple_of(i * PAD, 16), PAD)
            for p in range(3):
                q = qkv[r, 128 * p:128 * p + 128]
                k = qkv[r, D + 128 * p:D + 128 * p + 128]
                v = qkv[r, 2 * D + 128 * p:2 * D + 128 * p + 128]
                acc = None
                for h in range(2):
                    s = mm_nt(q, half(k, h))
                    s = jnp.where(keycol, s, -1e30)
                    e = jnp.exp(s - jnp.max(s, axis=-1, keepdims=True))
                    pr = (e * (1.0 / jnp.sum(e, axis=-1, keepdims=True))).astype(BF16)
                    ps[i * HEADS + 2 * p + h] = pr
                    o = mm(pr, half(v, h))
                    acc = o if acc is None else acc + o
                cs[r, 128 * p:128 * p + 128] = acc.astype(BF16)

    attention(0, 6)
    forward(2)
    attention(6, 12)
    forward(3)
    forward(4)
    for j in (2, 3, 4):
        gathered(j)

    @pl.loop(0, NI // CH2)
    def _(c):
        r = pl.ds(pl.multiple_of(c * (CH2 * PAD), 16), CH2 * PAD)
        xs = jnp.concatenate([padded(x_ref, c * CH2 + j, tmp) for j in range(CH2)], axis=0)
        x1 = xs + mm(cs[r, :], wo[...]) + vec(2)
        n2, rs2 = norm_parts(x1)
        h2 = (n2 * vec(3) + vec(4)).astype(BF16)
        h2s[r, :] = h2
        dy = dys[r, :]
        acc, dh = x1 + vec(5), None
        for f in range(4):
            fc = slice(f * D, f * D + D)
            u = mm(h2, wup[:, fc]) + vec(9 + f)
            g, gp = gelu_both(u)
            g = g.astype(BF16)
            gs[r, fc] = g
            acc = acc + mm(g, wd[fc, :])
            du = (mm_nt(dy, wd[fc, :]) * gp).astype(BF16)
            dus[r, fc] = du
            gvec[9 + f:10 + f, :] += colsum(du.astype(F32))
            o = mm_nt(du, wup[:, fc])
            dh = o if dh is None else dh + o
        for j in range(CH2):
            stage[c * CH2 + j] = acc[j * PAD:j * PAD + SEQ].astype(BF16)
        gvec[3:4, :] += colsum(dh * n2)
        gvec[4:5, :] += colsum(dh)
        dx1 = dy.astype(F32) + norm_back(dh * vec(3), n2, rs2)
        db = dx1.astype(BF16)
        dbs[r, :] = db
        gvec[2:3, :] += colsum(db.astype(F32))
        dys[r, :] = mm_nt(db, wo[...]).astype(BF16)

    out_copy = pltpu.make_async_copy(stage, out_ref, out_sem)
    out_copy.start()

    def put(value, row):
        value = value.astype(BF16)
        for s in range(4):
            for b in range(value.shape[1] // 128):
                r = pl.ds(pl.multiple_of(row + 96 * b, 16), 96)
                grads[s % 2, s // 2, r, :] = value[96 * s:96 * s + 96, 128 * b:128 * b + 128]

    @pl.loop(0, 2)
    def _(h):
        for core in range(2):
            cc = pl.ds(pl.multiple_of(h * 768 + core * 384, 128), 384)
            value = mm(dyT[...], gs[:, cc]).astype(BF16)
            for b in range(3):
                grads[core, h, DOWN_ROW + 384 * b:DOWN_ROW + 384 * b + 384, :] = value[:, 128 * b:128 * b + 128]

    transpose_into(tT, h2s)

    @pl.loop(0, 4)
    def _(n):
        cc = pl.ds(pl.multiple_of(n * 384, 128), 384)
        put(mm(tT[...], dus[:, cc]), UP_ROW + 288 * n)

    transpose_into(tT, cs)
    put(mm(tT[...], dbs[...]), OUT_ROW)
    red[0].send_core()
    transpose_into(tT, h1s)

    def attention_back(p):
        sl = [slice(j * D + 128 * p, j * D + 128 * p + 128) for j in range(3)]

        @pl.loop(0, NI)
        def _(i):
            r = pl.ds(pl.multiple_of(i * PAD, 16), PAD)
            q, k, v = (qkv[r, s] for s in sl)
            dc = dys[r, 128 * p:128 * p + 128]
            dq = dk = dv = None
            for h in range(2):
                pr = ps[i * HEADS + 2 * p + h]
                da = mm_nt(dc, half(v, h))
                prf = pr.astype(F32)
                t = prf * da
                ds = (t - prf * jnp.sum(t, axis=-1, keepdims=True)).astype(BF16)
                ov = mm_tn(pr, half(dc, h))
                oq = mm(ds, half(k, h))
                ok = mm_tn(ds, half(q, h))
                if dq is None:
                    dq, dk, dv = oq, ok, ov
                else:
                    dq, dk, dv = dq + oq, dk + ok, dv + ov
            for j, o in enumerate((dq * 0.125, dk, dv)):
                o = o.astype(BF16)
                qkv[r, sl[j]] = o
                if j != 1:
                    gvec[6 + j:7 + j, 128 * p:128 * p + 128] += colsum(o.astype(F32))

    def qkv_grad(p):
        rhs = jnp.concatenate([qkv[:, j * D + 128 * p:j * D + 128 * p + 128] for j in range(3)], axis=1)
        put(mm(tT[...], rhs), QKV_ROW + 288 * p)

    attention_back(0)
    red[0].send_planes()
    qkv_grad(0)
    attention_back(1)
    red[0].send_row()
    qkv_grad(1)
    red[1].send_core()
    attention_back(2)
    red[0].send_back()
    red[1].send_planes()
    qkv_grad(2)
    red[2].send_core()
    out_copy.wait()

    def first_norm_back(a, b):
        @pl.loop(a // CH4, b // CH4)
        def _(c):
            r = pl.ds(pl.multiple_of(c * (CH4 * PAD), 16), CH4 * PAD)
            dh = mm_nt(qkv[r, :], wqkv[...])
            xs = jnp.concatenate([padded(x_ref, c * CH4 + j, tmp) for j in range(CH4)], axis=0)
            n1, rs1 = norm_parts(xs)
            gvec[0:1, :] += colsum(dh * n1)
            gvec[1:2, :] += colsum(dh)
            ig = dbs[r, :].astype(F32) + norm_back(dh * vec(0), n1, rs1)
            for j in range(CH4):
                stage[c * CH4 + j] = ig[j * PAD:j * PAD + SEQ].astype(BF16)

    first_norm_back(0, 4)
    red[2].send_planes()
    first_norm_back(4, 8)
    red[1].send_row()
    first_norm_back(8, 12)

    ig_copy = pltpu.make_async_copy(stage, ig_ref, out_sem)
    ig_copy.start()
    gv = gvec[...]
    for s in range(4):
        moved = gv if s == 0 else pltpu.roll(gv, D - 96 * s, 1)
        bias = gv if s % 2 == 0 else pltpu.roll(gv, D - 192, 1)
        br = 6 if s < 2 else 8
        tile = jnp.concatenate(
            [moved[0:6, 0:128], bias[br:br + 1, 0:128], bias[br:br + 1, 128:256]]
            + [gv[9 + s:10 + s, 128 * b:128 * b + 128] for b in range(3)] + [jnp.zeros((5, 128), F32)],
            axis=0,
        )
        gradv[s % 2, s // 2] = tile.astype(BF16)
    redv.send_core()
    red[2].send_row()
    redv.send_planes()
    red[1].send_back()
    red[2].send_back()
    redv.send_row()
    for g in (0, 1, 2):
        red[g].finish()
    redv.send_back()
    fin_ref[...] = fin[...]
    finv_ref[...] = finv[...]
    for j in range(5):
        first[j].wait_send()
        second[j].wait_send()
        third[j].wait_send()
    ig_copy.wait()


def scratches():
    V = pltpu.VMEM
    bufs = []
    for n, full in ((160, 2560), (32, 512), (32, 512), (16, 16)):
        bufs += [V((2, full, 128), BF16), V((15, 2, n, 128), BF16), V((2, n, 128), BF16), V((3, n, 128), BF16)]
    return [
        V((NI, SEQ, D), BF16), pltpu.SemaphoreType.DMA,
        V((PAD, D), F32), V((TROWS, D), BF16), V((D, TROWS), BF16), V((D, TROWS), BF16),
        V((TROWS, D), BF16), V((TROWS, 3 * D), BF16), V((NI * HEADS, PAD, PAD), BF16),
        V((TROWS, D), BF16), V((TROWS, D), BF16), V((TROWS, FF), BF16), V((TROWS, FF), BF16),
        V((TROWS, D), BF16),
        V((64, D), BF16), V((D, 3 * D), BF16), V((D, D), BF16), V((D, FF), BF16), V((FF, D), BF16),
        V((16, D), F32), V((16, D), F32), V((2, 2, GROWS, 128), BF16), V((2, 2, 16, 128), BF16),
        *bufs,
        V((GROWS, 128), BF16), V((16, 128), BF16),
        pltpu.SemaphoreType.DMA((160,)), pltpu.SemaphoreType.DMA((160,)),
    ]


def layer(x, dy, vecs, wqkv, wo, wup, wd):
    S = jax.ShapeDtypeStruct
    vm, hbm = pl.BlockSpec(memory_space=pltpu.VMEM), pl.BlockSpec(memory_space=pl.ANY)
    return pl.pallas_call(
        body,
        out_shape=(S(x.shape, BF16), S(x.shape, BF16), S((GROWS, 128), BF16), S((16, 128), BF16)),
        in_specs=[vm, hbm] + [vm] * 5, out_specs=(hbm, hbm, vm, vm),
        scratch_shapes=scratches(),
        compiler_params=pltpu.CompilerParams(
            vmem_limit_bytes=int(63.5 * 2**20), collective_id=0, has_side_effects=True),
    )(x, dy, vecs, wqkv, wo, wup, wd)


def unpack_body(fin, finv, g1, s1, gqkv, gqv, go, bo, g2, s2, gup, bup, gd, bd):
    for b in range(12):
        gup[:, 128 * b:128 * b + 128] = fin[UP_ROW + 96 * b:UP_ROW + 96 * b + 96, :].astype(F32)
    for b in range(3):
        gd[128 * b:128 * b + 128, :] = fin[DOWN_ROW + 384 * b:DOWN_ROW + 384 * b + 384, :].astype(F32).T
        go[:, 128 * b:128 * b + 128] = fin[OUT_ROW + 96 * b:OUT_ROW + 96 * b + 96, :].astype(F32)
    for p in range(3):
        for j in range(3):
            r = QKV_ROW + 288 * p + 96 * j
            gqkv[:, j * D + 128 * p:j * D + 128 * p + 128] = fin[r:r + 96, :].astype(F32)
    v = finv[...].astype(F32)
    for row, ref in enumerate((g1, s1, bo, g2, s2, bd)):
        ref[...] = v[row, 0:96]
    gqv[0:128] = v[6, :]
    gqv[128:192] = v[7, 0:64]
    for b in range(3):
        bup[128 * b:128 * b + 128] = v[8 + b, :]


def unpack(fin, finv):
    def S(*shape):
        return jax.ShapeDtypeStruct(shape, F32)

    vm = pl.BlockSpec(memory_space=pltpu.VMEM)
    return pl.pallas_call(
        unpack_body,
        out_shape=(S(96), S(96), S(96, 3 * D), S(192), S(96, D), S(96), S(96), S(96),
                   S(96, FF), S(384), S(384, D), S(96)),
        in_specs=[vm] * 2, out_specs=(vm,) * 12,
        compiler_params=pltpu.CompilerParams(vmem_limit_bytes=24 * 2**20),
    )(fin, finv)


def local(inputs, out_grad, ln1_gain, ln1_shift, qkv_weight, qv_bias, out_weight, out_bias,
          ln2_gain, ln2_shift, up_weight, up_bias, down_weight, down_bias):
    shard = lax.axis_index("shard")
    lane = jnp.arange(D)
    six = jnp.stack([ln1_gain, ln1_shift, out_bias, ln2_gain, ln2_shift, down_bias])
    six = jnp.where(lane // 96 == shard, jnp.tile(six, (1, 4)), 0)
    two = jnp.where(lane // 192 == shard % 2, jnp.tile(qv_bias, 2), 0)
    row = jnp.arange(16)[:, None]
    vecs = jnp.concatenate([six, jnp.zeros((10, D), BF16)])
    vecs = jnp.where(row == 6 + 2 * (shard // 2), two, vecs)
    vecs = jnp.where(row == 9 + shard, up_bias, vecs)
    outputs, input_grad, fin, finv = layer(
        inputs, out_grad, vecs, qkv_weight, out_weight, up_weight, down_weight)
    return (outputs, input_grad, *unpack(fin, finv))


def solution(mesh):
    tokens, whole, rows = P(("rep", "shard"), None, None), P("shard"), P("shard", None)
    vectors = (whole, whole, rows, whole, rows, whole, whole, whole, rows, whole, rows, whole)
    return jax.shard_map(
        local, mesh=mesh, in_specs=(tokens, tokens, *vectors),
        out_specs=(tokens, tokens, *vectors), check_vma=False)
```

```python
import math

import jax
import jax.numpy as jnp
from jax import lax
from jax.experimental import pallas as pl
from jax.experimental.pallas import tpu as pltpu
from jax.sharding import PartitionSpec as P

NI, SEQ, D, FF, HEADS = 12, 197, 384, 1536, 6
PAD = 208
ROWS = NI * PAD
TROWS = 2560
F32, BF16 = jnp.float32, jnp.bfloat16


def mm(a, b):
    return lax.dot_general(a, b, (((1,), (0,)), ((), ())), preferred_element_type=F32)


def mm_nt(a, b):
    return lax.dot_general(a, b, (((1,), (1,)), ((), ())), preferred_element_type=F32)


def mm_tn(a, b):
    return lax.dot_general(a, b, (((0,), (0,)), ((), ())), preferred_element_type=F32)


def norm_parts(v):
    avg = jnp.mean(v, axis=-1, keepdims=True)
    cen = v - avg
    var = jnp.mean(cen * cen, axis=-1, keepdims=True)
    rs = lax.rsqrt(var + 1e-6)
    return cen * rs, rs


def norm_back(e, n, rs):
    return rs * (e - jnp.mean(e, axis=-1, keepdims=True) - n * jnp.mean(e * n, axis=-1, keepdims=True))


def gelu_both(u):
    phi = 0.5 + 0.5 * lax.erf(u * math.sqrt(0.5))
    e = jnp.exp2(u * u * (-0.5 * math.log2(math.e)))
    return u * phi, phi + u * (e * (1.0 / math.sqrt(2 * math.pi)))


def colsum(v):
    return jnp.sum(v, axis=0, keepdims=True)

CH1, CH2, CH4, FC = 2, 2, 2, 512
MESH = pl.DeviceIdType.MESH

DOWN_ROW, UP_ROW, OUT_ROW, QKV_ROW = 0, 1152, 2304, 2592
GROWS = 3584
GROUPS = ((0, 64), (1024, 96), (2560, 32), (3072, 32))


class Comm:
    def __init__(self, ssem, rsem):
        self.ssem, self.rsem = ssem, rsem
        rep, shard = lax.axis_index("rep"), lax.axis_index("shard")
        self.z, self.y, self.lo = rep // 8, (rep // 2) % 4, rep % 2
        self.hi, self.core, self.plane = shard // 2, shard % 2, rep // 2
        self.sibling = (rep, self.hi * 2 + 1 - self.core)
        self.across = (self.plane * 2 + 1 - self.lo, (1 - self.hi) * 2 + self.core)
        self.row = []
        for dh, dl in ((0, 1), (1, 0), (1, 1)):
            ph, plo = (self.hi + dh) % 2, (self.lo + dl) % 2
            self.row.append(((self.plane * 2 + plo, ph * 2 + self.core), ph))
        self.planes = []
        for d in range(1, 16):
            pz, py = (self.z + d // 4) % 4, (self.y + d % 4) % 4
            q = pz * 4 + py
            self.planes.append(((q * 2 + self.lo, shard), q))

    def barrier(self, meanwhile):
        sem = pltpu.get_barrier_semaphore()
        peers = [self.sibling] + [d for d, _ in self.row] + [d for d, _ in self.planes]
        for dev in peers:
            pl.semaphore_signal(sem, inc=1, device_id=dev, device_id_type=MESH)
        meanwhile()
        pl.semaphore_wait(sem, len(peers))

    def copy(self, src, dst, slot, dev):
        return pltpu.make_async_remote_copy(
            src_ref=src, dst_ref=dst, send_sem=self.ssem.at[slot], recv_sem=self.rsem.at[slot],
            device_id=dev, device_id_type=MESH,
        )


class Reduce:
    def __init__(self, comm, base, grads, fin, start, n, rcore, rplane, part, rrow, scatter=True):
        c = comm
        self.c, self.n, self.scatter, self.start = c, n, scatter, start
        total = 16 * n if scatter else n
        self.grads, self.rcore, self.rplane, self.part, self.rrow, self.fin = (
            grads, rcore, rplane, part, rrow, fin)
        self.total = total
        rows = pl.ds(start, total)
        self.rows = rows
        self.core_copy = c.copy(grads.at[1 - c.core, :, rows, :], rcore, base, c.sibling)

        def piece(q):
            return pl.ds(pl.multiple_of(start + q * n, 16), n) if scatter else rows

        self.piece = piece
        self.plane_copies = [
            c.copy(grads.at[c.core, :, piece(q), :], rplane.at[d], base + 1 + d, dev)
            for d, (dev, q) in enumerate(c.planes)
        ]
        self.row_copies = [
            c.copy(part.at[h], rrow.at[d], base + 16 + d, dev)
            for d, (dev, h) in enumerate(c.row)
        ]
        if scatter:
            mine = piece(c.plane)
            self.back_copies = [
                c.copy(fin.at[mine, :], fin.at[mine, :], base + 19 + d, dev)
                for d, (dev, q) in enumerate(c.planes)
            ]

    def send_core(self):
        self.core_copy.start()

    def send_planes(self):
        self.core_copy.wait()
        step = 256 if self.total % 256 == 0 else 16

        @pl.loop(0, self.total // step)
        def _(b):
            off = pl.multiple_of(b * step, 16)
            r = pl.ds(pl.multiple_of(self.start + off, 16), step)
            for h in range(2):
                s = self.grads[self.c.core, h, r, :].astype(F32) + self.rcore[h, pl.ds(off, step), :].astype(F32)
                self.grads[self.c.core, h, r, :] = s.astype(BF16)

        for cp in self.plane_copies:
            cp.start()

    def send_row(self):
        for cp in self.plane_copies:
            cp.wait()
        for h in range(2):
            s = self.grads[self.c.core, h, self.piece(self.c.plane), :].astype(F32)
            for d in range(15):
                s = s + self.rplane[d, h].astype(F32)
            self.part[h] = s.astype(BF16)
        for cp in self.row_copies:
            cp.start()

    def send_back(self):
        for cp in self.row_copies:
            cp.wait()
        s = self.part[self.c.hi].astype(F32)
        for d in range(3):
            s = s + self.rrow[d].astype(F32)
        if self.scatter:
            self.fin[self.piece(self.c.plane), :] = s.astype(BF16)
            for cp in self.back_copies:
                cp.start()
        else:
            self.fin[...] = s.astype(BF16)

    def finish(self):
        for cp in self.back_copies:
            cp.wait()


def padded(ref, i, tmp):
    tmp[0:SEQ, :] = ref[i].astype(F32)
    return tmp[...]


def body(x_ref, dy_ref, g1_in, s1_in, wqkv_in, qv_in, wo_in, bo_in, g2_in, s2_in, wup_in, bup_in,
         wd_in, bd_in,
         out_ref, ig_ref, fin_ref, finv_ref,
         stage, out_sem, packed, vin_ref, tmp, gub, dys, dyT, tT, h1s, qkv, ps, cs, h2s, gs, dus, dbs,
         vecs_all, wqkv, wo, wup, wd, vec_ref, gvec, grads, gradv,
         rcore0, rplane0, part0, rrow0, rcore1, rplane1, part1, rrow1,
         rcore2, rplane2, part2, rrow2, rcore3, rplane3, part3, rrow3, rcorev, rplanev, partv, rrowv, fin, finv, ssem, rsem):
    dy_copy = pltpu.make_async_copy(dy_ref, stage, out_sem)
    dy_copy.start()
    comm = Comm(ssem, rsem)
    shard = comm.hi * 2 + comm.core
    theirs = (1 - comm.hi) * 2 + comm.core

    def place(full, s):
        n = full.shape[0] // 4
        return full.at[pl.ds(pl.multiple_of(s * n, 16), n)]

    params = ((wqkv_in, wqkv), (vin_ref, vecs_all), (wo_in, wo), (wup_in, wup), (wd_in, wd))
    def meanwhile():
        packed[...] = jnp.zeros_like(packed)
        for row, ref in enumerate((g1_in, s1_in, bo_in, g2_in, s2_in, bd_in)):
            packed[row, 0:96] = ref[...].astype(F32)
        packed[6, 0:192] = qv_in[...].astype(F32)
        packed[7, :] = bup_in[...].astype(F32)
        row = lax.broadcasted_iota(jnp.int32, (16, 1), 0)
        own = packed[...]
        six = jnp.where(row < 6, pltpu.roll(own, 96 * shard, 1), 0.0)
        two = pltpu.roll(own, 192 * comm.core, 1)[6:7, :]
        two = jnp.where(row == 6 + 2 * comm.hi, two, 0.0)
        up = jnp.where(row == 9 + shard, own[7:8, :], 0.0)
        vin_ref[...] = (six + two + up).astype(BF16)
        for own, full in params:
            n = own.shape[0]
            full[pl.ds(pl.multiple_of(shard * n, 16), n), :] = own[...]
        tmp[...] = jnp.zeros_like(tmp)
        gvec[...] = jnp.zeros_like(gvec)
        gub[...] = jnp.zeros_like(gub)
        for t in (dys, h1s, cs, h2s, gs, dus, dbs, qkv):
            t[ROWS:TROWS, :] = jnp.zeros((TROWS - ROWS, t.shape[1]), t.dtype)
        grads[:, :, QKV_ROW + 864:, :] = jnp.zeros((2, 2, GROWS - QKV_ROW - 864, 128), BF16)
        dy_copy.wait()

        @pl.loop(0, NI)
        def _(i):
            r = pl.ds(pl.multiple_of(i * PAD, 16), PAD)
            dy = padded(stage, i, tmp)
            dys[r, :] = dy.astype(BF16)
            gvec[5:6, :] += colsum(dy)

    comm.barrier(meanwhile)
    first, second, third = [], [], []
    for j, (own, full) in enumerate(params):
        first.append(comm.copy(own, place(full, shard), 3 * j, comm.across))
        second.append(comm.copy(own, place(full, shard), 3 * j + 1, comm.sibling))
        third.append(comm.copy(place(full, theirs), place(full, theirs), 3 * j + 2, comm.sibling))

    def send(j):
        first[j].start()
        second[j].start()

    send(1)
    send(0)

    def forward(j):
        first[j].wait_recv()
        third[j].start()

    def gathered(j):
        second[j].wait_recv()
        third[j].wait_recv()

    red = [Reduce(comm, 16 + 40 * g, grads, fin, start, n, *bufs)
           for g, ((start, n), bufs) in enumerate(zip(GROUPS, (
               (rcore0, rplane0, part0, rrow0), (rcore1, rplane1, part1, rrow1),
               (rcore2, rplane2, part2, rrow2), (rcore3, rplane3, part3, rrow3))))]
    redv = Reduce(comm, 176, gradv, finv, 0, 16, rcorev, rplanev, partv, rrowv, scatter=False)

    def vec(r):
        return vec_ref[r:r + 1, :]

    def vcat(r, n):
        return jnp.concatenate([vec_ref[r + j:r + j + 1, :] for j in range(n)], axis=1)

    def transpose_into(dst, src):
        @pl.loop(0, TROWS // 256)
        def _(b):
            r = pl.ds(pl.multiple_of(b * 256, 256), 256)
            dst[:, r] = src[r, :].T

    transpose_into(dyT, dys)
    forward(1)
    gathered(1)
    vec_ref[...] = (
        vecs_all[0:16, :].astype(F32) + vecs_all[16:32, :].astype(F32)
        + vecs_all[32:48, :].astype(F32) + vecs_all[48:64, :].astype(F32)
    )

    def first_norm(a, b):
        @pl.loop(a, b)
        def _(i):
            r = pl.ds(pl.multiple_of(i * PAD, 16), PAD)
            n, _ = norm_parts(padded(x_ref, i, tmp))
            h1s[r, :] = (n * vec(0) + vec(1)).astype(BF16)

    first_norm(0, 9)
    forward(0)
    for j in (2, 3, 4):
        send(j)
    first_norm(9, 12)
    gathered(0)

    lane = lax.broadcasted_iota(jnp.int32, (1, 128), 1)
    halves = (lane < 64, lane >= 64)
    lastcol = lax.broadcasted_iota(jnp.int32, (1, PAD - 128), 1) < SEQ - 128
    zero = jnp.zeros((), BF16)

    def half(v, h):
        return jnp.where(halves[h], v, zero)

    @pl.loop(0, NI // CH1)
    def _(c):
        r = pl.ds(pl.multiple_of(c * (CH1 * PAD), 16), CH1 * PAD)
        p = mm(h1s[r, :], wqkv[...]) + vcat(6, 3)
        qkv[r, 0:D] = (p[:, 0:D] * 0.125).astype(BF16)
        qkv[r, D:3 * D] = p[:, D:].astype(BF16)

    def attention(first_image, last_image):
        @pl.loop(first_image, last_image)
        def _(i):
            r = pl.ds(pl.multiple_of(i * PAD, 16), PAD)
            q, k, v = ([qkv[r, j * D + 128 * p:j * D + 128 * p + 128] for p in range(3)] for j in range(3))
            ss = [mm_nt(q[h // 2], half(k[h // 2], h % 2)) for h in range(6)]
            pr = []
            for h in range(6):
                s = jnp.concatenate([ss[h][:, 0:128], jnp.where(lastcol, ss[h][:, 128:PAD], -1e30)], axis=1)
                e = jnp.exp(s - jnp.max(s, axis=-1, keepdims=True))
                pr.append((e * (1.0 / jnp.sum(e, axis=-1, keepdims=True))).astype(BF16))
                ps[i * HEADS + h] = pr[h]
            for p in range(3):
                acc = mm(pr[2 * p], half(v[p], 0)) + mm(pr[2 * p + 1], half(v[p], 1))
                cs[r, 128 * p:128 * p + 128] = acc.astype(BF16)

    attention(0, 9)
    forward(2)
    forward(3)
    attention(9, 12)
    forward(4)
    for j in (2, 3, 4):
        gathered(j)

    @pl.loop(0, NI // CH2)
    def _(c):
        r = pl.ds(pl.multiple_of(c * (CH2 * PAD), 16), CH2 * PAD)
        xs = jnp.concatenate([padded(x_ref, c * CH2 + j, tmp) for j in range(CH2)], axis=0)
        x1 = xs + mm(cs[r, :], wo[...]) + vec(2)
        n2, rs2 = norm_parts(x1)
        h2 = (n2 * vec(3) + vec(4)).astype(BF16)
        h2s[r, :] = h2
        dy = dys[r, :]
        bup = vcat(9, 4)
        acc, dh = x1 + vec(5), None
        for f in range(FF // FC):
            fc = slice(f * FC, f * FC + FC)
            u = mm(h2, wup[:, fc]) + bup[:, fc]
            g, gp = gelu_both(u)
            g = g.astype(BF16)
            gs[r, fc] = g
            acc = acc + mm(g, wd[fc, :])
            du = (mm_nt(dy, wd[fc, :]) * gp).astype(BF16)
            dus[r, fc] = du
            gub[0:1, fc] += colsum(du.astype(F32))
            o = mm_nt(du, wup[:, fc])
            dh = o if dh is None else dh + o
        for j in range(CH2):
            stage[c * CH2 + j] = acc[j * PAD:j * PAD + SEQ].astype(BF16)
        gvec[3:4, :] += colsum(dh * n2)
        gvec[4:5, :] += colsum(dh)
        dx1 = dy.astype(F32) + norm_back(dh * vec(3), n2, rs2)
        db = dx1.astype(BF16)
        dbs[r, :] = db
        gvec[2:3, :] += colsum(db.astype(F32))
        dys[r, :] = mm_nt(db, wo[...]).astype(BF16)

    out_copy = pltpu.make_async_copy(stage, out_ref, out_sem)
    out_copy.start()

    def put(value, row):
        value = value.astype(BF16)
        for s in range(4):
            for b in range(value.shape[1] // 128):
                r = pl.ds(pl.multiple_of(row + 96 * b, 16), 96)
                grads[s % 2, s // 2, r, :] = value[96 * s:96 * s + 96, 128 * b:128 * b + 128]

    @pl.loop(0, 2)
    def _(h):
        for core in range(2):
            cc = pl.ds(pl.multiple_of(h * 768 + core * 384, 128), 384)
            value = mm(dyT[...], gs[:, cc]).astype(BF16)
            for b in range(3):
                grads[core, h, DOWN_ROW + 384 * b:DOWN_ROW + 384 * b + 384, :] = value[:, 128 * b:128 * b + 128]

    red[0].send_core()
    transpose_into(tT, h2s)

    @pl.loop(0, FF // FC)
    def _(n):
        cc = pl.ds(pl.multiple_of(n * FC, 128), FC)
        put(mm(tT[...], dus[:, cc]), UP_ROW + 3 * FC // 4 * n)

    red[0].send_planes()

    transpose_into(tT, cs)
    put(mm(tT[...], dbs[...]), OUT_ROW)
    red[1].send_core()
    transpose_into(tT, h1s)

    def attention_back(p):
        sl = [slice(j * D + 128 * p, j * D + 128 * p + 128) for j in range(3)]

        @pl.loop(0, NI // 3)
        def _(c):
            rs = [pl.ds(pl.multiple_of((3 * c + m) * PAD, 16), PAD) for m in range(3)]
            q, k, v = ([qkv[r, t] for r in rs] for t in sl)
            dc = [dys[r, 128 * p:128 * p + 128] for r in rs]
            pr = [ps.at[(3 * c + m) * HEADS + 2 * p + h] for m in range(3) for h in range(2)]
            das = [mm_nt(dc[m // 2], half(v[m // 2], m % 2)) for m in range(6)]
            dss = []
            for m in range(6):
                prf = pr[m][...].astype(F32)
                t = prf * das[m]
                dss.append((t - prf * jnp.sum(t, axis=-1, keepdims=True)).astype(BF16))
            for m in range(3):
                a, b = 2 * m, 2 * m + 1
                dv = mm_tn(pr[a][...], half(dc[m], 0)) + mm_tn(pr[b][...], half(dc[m], 1))
                dq = mm(dss[a], half(k[m], 0)) + mm(dss[b], half(k[m], 1))
                dk = mm_tn(dss[a], half(q[m], 0)) + mm_tn(dss[b], half(q[m], 1))
                for j, o in enumerate((dq * 0.125, dk, dv)):
                    o = o.astype(BF16)
                    qkv[rs[m], sl[j]] = o
                    if j != 1:
                        gvec[6 + j:7 + j, 128 * p:128 * p + 128] += colsum(o.astype(F32))

    def qkv_grad(p):
        rhs = jnp.concatenate([qkv[:, j * D + 128 * p:j * D + 128 * p + 128] for j in range(3)], axis=1)
        put(mm(tT[...], rhs), QKV_ROW + 288 * p)

    attention_back(0)
    red[1].send_planes()
    qkv_grad(0)
    attention_back(1)
    red[0].send_row()
    qkv_grad(1)
    red[2].send_core()
    attention_back(2)
    red[0].send_back()
    red[2].send_planes()
    qkv_grad(2)
    red[3].send_core()
    red[1].send_row()
    out_copy.wait()

    def first_norm_back(a, b):
        @pl.loop(a // CH4, b // CH4)
        def _(c):
            r = pl.ds(pl.multiple_of(c * (CH4 * PAD), 16), CH4 * PAD)
            dh = mm_nt(qkv[r, :], wqkv[...])
            xs = jnp.concatenate([padded(x_ref, c * CH4 + j, tmp) for j in range(CH4)], axis=0)
            n1, rs1 = norm_parts(xs)
            gvec[0:1, :] += colsum(dh * n1)
            gvec[1:2, :] += colsum(dh)
            ig = dbs[r, :].astype(F32) + norm_back(dh * vec(0), n1, rs1)
            for j in range(CH4):
                stage[c * CH4 + j] = ig[j * PAD:j * PAD + SEQ].astype(BF16)

    first_norm_back(0, 4)
    red[3].send_planes()
    first_norm_back(4, 8)
    red[1].send_back()
    red[2].send_row()
    first_norm_back(8, 12)

    ig_copy = pltpu.make_async_copy(stage, ig_ref, out_sem)
    ig_copy.start()
    for b in range(4):
        gvec[9 + b:10 + b, :] = gub[0:1, b * D:b * D + D]
    gv = gvec[...]
    for s in range(4):
        moved = gv if s == 0 else pltpu.roll(gv, D - 96 * s, 1)
        bias = gv if s % 2 == 0 else pltpu.roll(gv, D - 192, 1)
        br = 6 if s < 2 else 8
        tile = jnp.concatenate(
            [moved[0:6, 0:128], bias[br:br + 1, 0:128], bias[br:br + 1, 128:256]]
            + [gv[9 + s:10 + s, 128 * b:128 * b + 128] for b in range(3)] + [jnp.zeros((5, 128), F32)],
            axis=0,
        )
        gradv[s % 2, s // 2] = tile.astype(BF16)
    redv.send_core()
    red[3].send_row()
    redv.send_planes()
    red[2].send_back()
    red[3].send_back()
    redv.send_row()
    for g in range(4):
        red[g].finish()
    redv.send_back()
    fin_ref[...] = fin[...]
    finv_ref[...] = finv[...]
    for j in range(5):
        first[j].wait_send()
        second[j].wait_send()
        third[j].wait_send()
    ig_copy.wait()


def scratches():
    V = pltpu.VMEM
    bufs = []
    for n, full in ((64, 1024), (96, 1536), (32, 512), (32, 512), (16, 16)):
        bufs += [V((2, full, 128), BF16), V((15, 2, n, 128), BF16), V((2, n, 128), BF16), V((3, n, 128), BF16)]
    return [
        V((NI, SEQ, D), BF16), pltpu.SemaphoreType.DMA,
        V((16, D), F32), V((16, D), BF16), V((PAD, D), F32), V((8, FF), F32), V((TROWS, D), BF16), V((D, TROWS), BF16), V((D, TROWS), BF16),
        V((TROWS, D), BF16), V((TROWS, 3 * D), BF16), V((NI * HEADS, PAD, PAD), BF16),
        V((TROWS, D), BF16), V((TROWS, D), BF16), V((TROWS, FF), BF16), V((TROWS, FF), BF16),
        V((TROWS, D), BF16),
        V((64, D), BF16), V((D, 3 * D), BF16), V((D, D), BF16), V((D, FF), BF16), V((FF, D), BF16),
        V((16, D), F32), V((16, D), F32), V((2, 2, GROWS, 128), BF16), V((2, 2, 16, 128), BF16),
        *bufs,
        V((GROWS, 128), BF16), V((16, 128), BF16),
        pltpu.SemaphoreType.DMA((200,)), pltpu.SemaphoreType.DMA((200,)),
    ]


def layer(x, dy, *params):
    S = jax.ShapeDtypeStruct
    vm, hbm = pl.BlockSpec(memory_space=pltpu.VMEM), pl.BlockSpec(memory_space=pl.ANY)
    return pl.pallas_call(
        body,
        out_shape=(S(x.shape, BF16), S(x.shape, BF16), S((GROWS, 128), BF16), S((16, 128), BF16)),
        in_specs=[vm, hbm] + [vm] * 12, out_specs=(hbm, hbm, vm, vm),
        scratch_shapes=scratches(),
        compiler_params=pltpu.CompilerParams(
            vmem_limit_bytes=int(63.5 * 2**20), collective_id=0, has_side_effects=True),
    )(x, dy, *params)


def unpack_body(out_in, ig_in, fin, finv, out, ig, g1, s1, gqkv, gqv, go, bo, g2, s2, gup, bup, gd, bd, sems):
    copies = [pltpu.make_async_copy(out_in, out, sems.at[0]), pltpu.make_async_copy(ig_in, ig, sems.at[1])]
    for copy in copies:
        copy.start()
    for b in range(12):
        gup[:, 128 * b:128 * b + 128] = fin[UP_ROW + 96 * b:UP_ROW + 96 * b + 96, :].astype(F32)
    for b in range(3):
        gd[128 * b:128 * b + 128, :] = fin[DOWN_ROW + 384 * b:DOWN_ROW + 384 * b + 384, :].astype(F32).T
        go[:, 128 * b:128 * b + 128] = fin[OUT_ROW + 96 * b:OUT_ROW + 96 * b + 96, :].astype(F32)
    for p in range(3):
        for j in range(3):
            r = QKV_ROW + 288 * p + 96 * j
            gqkv[:, j * D + 128 * p:j * D + 128 * p + 128] = fin[r:r + 96, :].astype(F32)
    v = finv[...].astype(F32)
    for row, ref in enumerate((g1, s1, bo, g2, s2, bd)):
        ref[...] = v[row, 0:96]
    gqv[0:128] = v[6, :]
    gqv[128:192] = v[7, 0:64]
    for b in range(3):
        bup[128 * b:128 * b + 128] = v[8 + b, :]
    for copy in copies:
        copy.wait()


def unpack(outputs, input_grad, fin, finv):
    def S(*shape):
        return jax.ShapeDtypeStruct(shape, F32)

    vm, hbm = pl.BlockSpec(memory_space=pltpu.VMEM), pl.BlockSpec(memory_space=pl.ANY)
    whole = jax.ShapeDtypeStruct(outputs.shape, BF16)
    return pl.pallas_call(
        unpack_body,
        out_shape=(whole, whole, S(96), S(96), S(96, 3 * D), S(192), S(96, D), S(96), S(96), S(96),
                   S(96, FF), S(384), S(384, D), S(96)),
        in_specs=[hbm, hbm, vm, vm], out_specs=(hbm, hbm) + (vm,) * 12,
        scratch_shapes=[pltpu.SemaphoreType.DMA((2,))],
        compiler_params=pltpu.CompilerParams(vmem_limit_bytes=24 * 2**20),
    )(outputs, input_grad, fin, finv)


def local(*arrays):
    return unpack(*layer(*arrays))


def solution(mesh):
    tokens, whole, rows = P(("rep", "shard"), None, None), P("shard"), P("shard", None)
    vectors = (whole, whole, rows, whole, rows, whole, whole, whole, rows, whole, rows, whole)
    return jax.shard_map(
        local, mesh=mesh, in_specs=(tokens, tokens, *vectors),
        out_specs=(tokens, tokens, *vectors), check_vma=False)
```

```python
import math

import jax
import jax.numpy as jnp
from jax import lax
from jax.experimental import pallas as pl
from jax.experimental.pallas import tpu as pltpu
from jax.sharding import PartitionSpec as P

NI, SEQ, D, FF, HEADS = 12, 197, 384, 1536, 6
PAD = 208
ROWS = NI * PAD
TROWS = 2560
F32, BF16 = jnp.float32, jnp.bfloat16


def mm(a, b):
    return lax.dot_general(a, b, (((1,), (0,)), ((), ())), preferred_element_type=F32)


def mm_nt(a, b):
    return lax.dot_general(a, b, (((1,), (1,)), ((), ())), preferred_element_type=F32)


def mm_tn(a, b):
    return lax.dot_general(a, b, (((0,), (0,)), ((), ())), preferred_element_type=F32)


def norm_parts(v):
    avg = jnp.mean(v, axis=-1, keepdims=True)
    cen = v - avg
    var = jnp.mean(cen * cen, axis=-1, keepdims=True)
    rs = lax.rsqrt(var + 1e-6)
    return cen * rs, rs


def norm_back(e, n, rs):
    return rs * (e - jnp.mean(e, axis=-1, keepdims=True) - n * jnp.mean(e * n, axis=-1, keepdims=True))


def gelu_both(u):
    phi = 0.5 + 0.5 * lax.erf(u * math.sqrt(0.5))
    e = jnp.exp2(u * u * (-0.5 * math.log2(math.e)))
    return u * phi, phi + u * (e * (1.0 / math.sqrt(2 * math.pi)))


def colsum(v):
    return jnp.sum(v, axis=0, keepdims=True)

CH1, CH2, CH4, FC = 2, 2, 2, 512
MESH = pl.DeviceIdType.MESH

DOWN_ROW, UP_ROW, OUT_ROW, QKV_ROW = 0, 1152, 2304, 2592
GROWS = 3584
SPREAD = ((0, 32), (1024, 48), (2560, 16))
LAST = (3072, 32)


class Comm:
    def __init__(self, ssem, rsem):
        self.ssem, self.rsem = ssem, rsem
        rep, shard = lax.axis_index("rep"), lax.axis_index("shard")
        self.z, self.y, self.lo = rep // 8, (rep // 2) % 4, rep % 2
        self.hi, self.core, self.plane = shard // 2, shard % 2, rep // 2
        self.sibling = (rep, self.hi * 2 + 1 - self.core)
        self.across = (self.plane * 2 + 1 - self.lo, (1 - self.hi) * 2 + self.core)
        self.mate = (self.plane * 2 + 1 - self.lo, shard)
        self.row, self.quarters = [], []
        for dh, dl in ((0, 1), (1, 0), (1, 1)):
            ph, plo = (self.hi + dh) % 2, (self.lo + dl) % 2
            dev = (self.plane * 2 + plo, ph * 2 + self.core)
            self.row.append((dev, ph))
            self.quarters.append((dev, ph, plo))
        self.planes = []
        for d in range(1, 16):
            pz, py = (self.z + d // 4) % 4, (self.y + d % 4) % 4
            q = pz * 4 + py
            self.planes.append(((q * 2 + self.lo, shard), q))

    def barrier(self, meanwhile):
        sem = pltpu.get_barrier_semaphore()
        peers = [self.sibling] + [d for d, _ in self.row] + [d for d, _ in self.planes]
        for dev in peers:
            pl.semaphore_signal(sem, inc=1, device_id=dev, device_id_type=MESH)
        meanwhile()
        pl.semaphore_wait(sem, len(peers))

    def copy(self, src, dst, slot, dev):
        return pltpu.make_async_remote_copy(
            src_ref=src, dst_ref=dst, send_sem=self.ssem.at[slot], recv_sem=self.rsem.at[slot],
            device_id=dev, device_id_type=MESH,
        )


class Reduce:
    def __init__(self, comm, base, grads, fin, start, n, rcore, rplane, part, rrow, scatter=True):
        c = comm
        self.c, self.n, self.scatter, self.start = c, n, scatter, start
        total = 16 * n if scatter else n
        self.grads, self.rcore, self.rplane, self.part, self.rrow, self.fin = (
            grads, rcore, rplane, part, rrow, fin)
        self.total = total
        rows = pl.ds(start, total)
        self.rows = rows
        self.core_copy = c.copy(grads.at[1 - c.core, :, rows, :], rcore, base, c.sibling)

        def piece(q):
            return pl.ds(pl.multiple_of(start + q * n, 16), n) if scatter else rows

        self.piece = piece
        self.plane_copies = [
            c.copy(grads.at[c.core, :, piece(q), :], rplane.at[d], base + 1 + d, dev)
            for d, (dev, q) in enumerate(c.planes)
        ]
        self.row_copies = [
            c.copy(part.at[h], rrow.at[d], base + 16 + d, dev)
            for d, (dev, h) in enumerate(c.row)
        ]
        if scatter:
            mine = piece(c.plane)
            self.back_copies = [
                c.copy(fin.at[mine, :], fin.at[mine, :], base + 19 + d, dev)
                for d, (dev, q) in enumerate(c.planes)
            ]

    def send_core(self):
        self.core_copy.start()

    def send_planes(self):
        self.core_copy.wait()
        step = 256 if self.total % 256 == 0 else 16

        @pl.loop(0, self.total // step)
        def _(b):
            off = pl.multiple_of(b * step, 16)
            r = pl.ds(pl.multiple_of(self.start + off, 16), step)
            for h in range(2):
                s = self.grads[self.c.core, h, r, :].astype(F32) + self.rcore[h, pl.ds(off, step), :].astype(F32)
                self.grads[self.c.core, h, r, :] = s.astype(BF16)

        for cp in self.plane_copies:
            cp.start()

    def send_row(self):
        for cp in self.plane_copies:
            cp.wait()
        for h in range(2):
            s = self.grads[self.c.core, h, self.piece(self.c.plane), :].astype(F32)
            for d in range(15):
                s = s + self.rplane[d, h].astype(F32)
            self.part[h] = s.astype(BF16)
        for cp in self.row_copies:
            cp.start()

    def send_back(self):
        for cp in self.row_copies:
            cp.wait()
        s = self.part[self.c.hi].astype(F32)
        for d in range(3):
            s = s + self.rrow[d].astype(F32)
        if self.scatter:
            self.fin[self.piece(self.c.plane), :] = s.astype(BF16)
            for cp in self.back_copies:
                cp.start()
        else:
            self.fin[...] = s.astype(BF16)

    def finish(self):
        for cp in self.back_copies:
            cp.wait()


class Spread:
    def __init__(self, comm, base, grads, fin, start, m, rcore, rrow, rplane):
        c = self.c = comm
        self.grads, self.fin, self.rcore, self.rrow, self.rplane = grads, fin, rcore, rrow, rplane
        self.start, self.half = start, 16 * m
        self.core_copy = c.copy(grads.at[1 - c.core, :, pl.ds(start, 32 * m), :], rcore, base, c.sibling)

        def rows(lo):
            return pl.ds(pl.multiple_of(start + lo * self.half, 16), self.half)

        def piece(q):
            return pl.ds(pl.multiple_of(start + c.lo * self.half + q * m, 16), m)

        self.rows, self.mine = rows, piece(c.plane)
        self.row_copies = [
            c.copy(grads.at[c.core, h, rows(lo), :], rrow.at[d], base + 1 + d, dev)
            for d, (dev, h, lo) in enumerate(c.quarters)
        ]
        self.plane_copies = [
            c.copy(grads.at[c.core, c.hi, piece(q), :], rplane.at[d], base + 4 + d, dev)
            for d, (dev, q) in enumerate(c.planes)
        ]
        self.back_copies = [
            c.copy(fin.at[self.mine, :], fin.at[self.mine, :], base + 19 + d, dev)
            for d, (dev, q) in enumerate(c.planes)
        ]
        self.mate_copy = c.copy(fin.at[rows(c.lo), :], fin.at[rows(c.lo), :], base + 34, c.mate)

    def send_core(self):
        self.core_copy.start()

    def send_row(self):
        self.core_copy.wait()

        @pl.loop(0, 2 * self.half // 256)
        def _(b):
            off = pl.multiple_of(b * 256, 256)
            r = pl.ds(pl.multiple_of(self.start + off, 16), 256)
            for h in range(2):
                t = self.grads[self.c.core, h, r, :].astype(F32) + self.rcore[h, pl.ds(off, 256), :].astype(F32)
                self.grads[self.c.core, h, r, :] = t.astype(BF16)

        for cp in self.row_copies:
            cp.start()

    def send_planes(self):
        for cp in self.row_copies:
            cp.wait()

        @pl.loop(0, self.half // 256)
        def _(b):
            off = pl.multiple_of(b * 256, 256)
            r = pl.ds(pl.multiple_of(self.start + self.c.lo * self.half + off, 16), 256)
            t = self.grads[self.c.core, self.c.hi, r, :].astype(F32)
            for d in range(3):
                t = t + self.rrow[d, pl.ds(off, 256), :].astype(F32)
            self.grads[self.c.core, self.c.hi, r, :] = t.astype(BF16)

        for cp in self.plane_copies:
            cp.start()

    def send_back(self):
        for cp in self.plane_copies:
            cp.wait()
        t = self.grads[self.c.core, self.c.hi, self.mine, :].astype(F32)
        for d in range(15):
            t = t + self.rplane[d].astype(F32)
        self.fin[self.mine, :] = t.astype(BF16)
        for cp in self.back_copies:
            cp.start()

    def send_mate(self):
        for cp in self.back_copies:
            cp.wait()
        self.mate_copy.start()

    def finish(self):
        self.mate_copy.wait()


def padded(ref, i, tmp):
    tmp[0:SEQ, :] = ref[i].astype(F32)
    return tmp[...]


def body(x_ref, dy_ref, g1_in, s1_in, wqkv_in, qv_in, wo_in, bo_in, g2_in, s2_in, wup_in, bup_in,
         wd_in, bd_in,
         out_ref, ig_ref, fin_ref, finv_ref,
         stage, out_sem, out_sem2, packed, vin_ref, tmp, gub, dys, dyT, tT, h1s, qkv, ps, cs, h2s, gs, dus, dbs,
         vecs_all, wqkv, wo, wup, wd, vec_ref, gvec, grads, gradv,
         rcore0, rrow0, rplane0, rcore1, rrow1, rplane1, rcore2, rrow2, rplane2,
         rcore3, rplane3, part3, rrow3, rcorev, rplanev, partv, rrowv, fin, finv, ssem, rsem):
    dy_copy = pltpu.make_async_copy(dy_ref, stage, out_sem)
    dy_copy.start()
    comm = Comm(ssem, rsem)
    shard = comm.hi * 2 + comm.core
    theirs = (1 - comm.hi) * 2 + comm.core

    def place(full, s):
        n = full.shape[0] // 4
        return full.at[pl.ds(pl.multiple_of(s * n, 16), n)]

    params = ((wqkv_in, wqkv), (vin_ref, vecs_all), (wo_in, wo), (wup_in, wup), (wd_in, wd))
    def meanwhile():
        packed[...] = jnp.zeros_like(packed)
        for row, ref in enumerate((g1_in, s1_in, bo_in, g2_in, s2_in, bd_in)):
            packed[row, 0:96] = ref[...].astype(F32)
        packed[6, 0:192] = qv_in[...].astype(F32)
        packed[7, :] = bup_in[...].astype(F32)
        row = lax.broadcasted_iota(jnp.int32, (16, 1), 0)
        own = packed[...]
        six = jnp.where(row < 6, pltpu.roll(own, 96 * shard, 1), 0.0)
        two = pltpu.roll(own, 192 * comm.core, 1)[6:7, :]
        two = jnp.where(row == 6 + 2 * comm.hi, two, 0.0)
        up = jnp.where(row == 9 + shard, own[7:8, :], 0.0)
        vin_ref[...] = (six + two + up).astype(BF16)
        for own, full in params:
            n = own.shape[0]
            full[pl.ds(pl.multiple_of(shard * n, 16), n), :] = own[...]
        tmp[...] = jnp.zeros_like(tmp)
        gvec[...] = jnp.zeros_like(gvec)
        gub[...] = jnp.zeros_like(gub)
        for t in (dys, h1s, cs, h2s, gs, dus, dbs, qkv):
            t[ROWS:TROWS, :] = jnp.zeros((TROWS - ROWS, t.shape[1]), t.dtype)
        grads[:, :, QKV_ROW + 864:, :] = jnp.zeros((2, 2, GROWS - QKV_ROW - 864, 128), BF16)
        dy_copy.wait()

        @pl.loop(0, NI)
        def _(i):
            r = pl.ds(pl.multiple_of(i * PAD, 16), PAD)
            dy = padded(stage, i, tmp)
            dys[r, :] = dy.astype(BF16)
            gvec[5:6, :] += colsum(dy)

    comm.barrier(meanwhile)
    first, second, third, mate, fourth = [], [], [], [], []
    for j, (own, full) in enumerate(params):
        n = own.shape[0]
        m = n // 2 if j != 1 else n

        def part(ref, s, which):
            return ref.at[pl.ds(pl.multiple_of(s * n + which * m, 16), m)]

        out_half, in_half = (1 - comm.lo, comm.lo) if j != 1 else (0, 0)
        first.append(comm.copy(part(own, 0, out_half), part(full, shard, out_half), 5 * j, comm.across))
        second.append(comm.copy(own, place(full, shard), 5 * j + 1, comm.sibling))
        mine, other = part(full, theirs, in_half), part(full, theirs, 1 - in_half)
        third.append(comm.copy(mine, mine, 5 * j + 2, comm.sibling))
        if j != 1:
            mate.append(comm.copy(mine, mine, 5 * j + 3, comm.mate))
            fourth.append(comm.copy(other, other, 5 * j + 4, comm.sibling))
        else:
            mate.append(None)
            fourth.append(None)

    def send(j):
        first[j].start()
        second[j].start()

    send(1)
    send(0)

    def forward(j):
        first[j].wait_recv()
        third[j].start()
        if j != 1:
            mate[j].start()

    def forward_mate(j):
        mate[j].wait_recv()
        fourth[j].start()

    def gathered(j):
        second[j].wait_recv()
        third[j].wait_recv()
        if j != 1:
            fourth[j].wait_recv()

    red = [
        Spread(comm, 25 + 35 * g, grads, fin, start, m, *bufs)
        for g, ((start, m), bufs) in enumerate(zip(SPREAD, (
            (rcore0, rrow0, rplane0), (rcore1, rrow1, rplane1), (rcore2, rrow2, rplane2))))
    ]
    red.append(Reduce(comm, 130, grads, fin, *LAST, rcore3, rplane3, part3, rrow3))
    redv = Reduce(comm, 166, gradv, finv, 0, 16, rcorev, rplanev, partv, rrowv, scatter=False)

    def vec(r):
        return vec_ref[r:r + 1, :]

    def vcat(r, n):
        return jnp.concatenate([vec_ref[r + j:r + j + 1, :] for j in range(n)], axis=1)

    def transpose_into(dst, src):
        @pl.loop(0, TROWS // 256)
        def _(b):
            r = pl.ds(pl.multiple_of(b * 256, 256), 256)
            dst[:, r] = src[r, :].T

    transpose_into(dyT, dys)
    forward(1)
    gathered(1)
    vec_ref[...] = (
        vecs_all[0:16, :].astype(F32) + vecs_all[16:32, :].astype(F32)
        + vecs_all[32:48, :].astype(F32) + vecs_all[48:64, :].astype(F32)
    )

    def first_norm(a, b):
        @pl.loop(a, b)
        def _(i):
            r = pl.ds(pl.multiple_of(i * PAD, 16), PAD)
            n, _ = norm_parts(padded(x_ref, i, tmp))
            h1s[r, :] = (n * vec(0) + vec(1)).astype(BF16)

    first_norm(0, 6)
    forward(0)
    for j in (2, 3, 4):
        send(j)
    first_norm(6, 12)
    forward_mate(0)
    gathered(0)

    lane = lax.broadcasted_iota(jnp.int32, (1, 128), 1)
    halves = (lane < 64, lane >= 64)
    lastcol = lax.broadcasted_iota(jnp.int32, (1, PAD - 128), 1) < SEQ - 128
    zero = jnp.zeros((), BF16)

    def half(v, h):
        return jnp.where(halves[h], v, zero)

    @pl.loop(0, NI // CH1)
    def _(c):
        r = pl.ds(pl.multiple_of(c * (CH1 * PAD), 16), CH1 * PAD)
        p = mm(h1s[r, :], wqkv[...]) + vcat(6, 3)
        qkv[r, 0:D] = (p[:, 0:D] * 0.125).astype(BF16)
        qkv[r, D:3 * D] = p[:, D:].astype(BF16)

    def attention(first_image, last_image):
        @pl.loop(first_image, last_image)
        def _(i):
            r = pl.ds(pl.multiple_of(i * PAD, 16), PAD)
            q, k, v = ([qkv[r, j * D + 128 * p:j * D + 128 * p + 128] for p in range(3)] for j in range(3))
            ss = [mm_nt(q[h // 2], half(k[h // 2], h % 2)) for h in range(6)]
            pr = []
            for h in range(6):
                s = jnp.concatenate([ss[h][:, 0:128], jnp.where(lastcol, ss[h][:, 128:PAD], -1e30)], axis=1)
                e = jnp.exp(s - jnp.max(s, axis=-1, keepdims=True))
                pr.append((e * (1.0 / jnp.sum(e, axis=-1, keepdims=True))).astype(BF16))
                ps[i * HEADS + h] = pr[h]
            for p in range(3):
                acc = mm(pr[2 * p], half(v[p], 0)) + mm(pr[2 * p + 1], half(v[p], 1))
                cs[r, 128 * p:128 * p + 128] = acc.astype(BF16)

    attention(0, 2)
    forward(2)
    forward(3)
    attention(2, 4)
    forward(4)
    attention(4, 7)
    forward_mate(2)
    forward_mate(3)
    attention(7, 10)
    forward_mate(4)
    attention(10, 12)
    for j in (2, 3, 4):
        gathered(j)

    @pl.loop(0, NI // CH2)
    def _(c):
        r = pl.ds(pl.multiple_of(c * (CH2 * PAD), 16), CH2 * PAD)
        xs = jnp.concatenate([padded(x_ref, c * CH2 + j, tmp) for j in range(CH2)], axis=0)
        x1 = xs + mm(cs[r, :], wo[...]) + vec(2)
        n2, rs2 = norm_parts(x1)
        h2 = (n2 * vec(3) + vec(4)).astype(BF16)
        h2s[r, :] = h2
        dy = dys[r, :]
        bup = vcat(9, 4)
        acc, dh = x1 + vec(5), None
        for f in range(FF // FC):
            fc = slice(f * FC, f * FC + FC)
            u = mm(h2, wup[:, fc]) + bup[:, fc]
            g, gp = gelu_both(u)
            g = g.astype(BF16)
            gs[r, fc] = g
            acc = acc + mm(g, wd[fc, :])
            du = (mm_nt(dy, wd[fc, :]) * gp).astype(BF16)
            dus[r, fc] = du
            gub[0:1, fc] += colsum(du.astype(F32))
            o = mm_nt(du, wup[:, fc])
            dh = o if dh is None else dh + o
        for j in range(CH2):
            stage[c * CH2 + j] = acc[j * PAD:j * PAD + SEQ].astype(BF16)
        gvec[3:4, :] += colsum(dh * n2)
        gvec[4:5, :] += colsum(dh)
        dx1 = dy.astype(F32) + norm_back(dh * vec(3), n2, rs2)
        db = dx1.astype(BF16)
        dbs[r, :] = db
        gvec[2:3, :] += colsum(db.astype(F32))
        dys[r, :] = mm_nt(db, wo[...]).astype(BF16)

    out_copy = pltpu.make_async_copy(stage, out_ref, out_sem)
    out_copy.start()

    def put(value, row):
        value = value.astype(BF16)
        for s in range(4):
            for b in range(value.shape[1] // 128):
                r = pl.ds(pl.multiple_of(row + 96 * b, 16), 96)
                grads[s % 2, s // 2, r, :] = value[96 * s:96 * s + 96, 128 * b:128 * b + 128]

    @pl.loop(0, 2)
    def _(h):
        for core in range(2):
            cc = pl.ds(pl.multiple_of(h * 768 + core * 384, 128), 384)
            value = mm(dyT[...], gs[:, cc]).astype(BF16)
            for b in range(3):
                grads[core, h, DOWN_ROW + 384 * b:DOWN_ROW + 384 * b + 384, :] = value[:, 128 * b:128 * b + 128]

    red[0].send_core()
    transpose_into(tT, h2s)

    @pl.loop(0, FF // FC)
    def _(n):
        cc = pl.ds(pl.multiple_of(n * FC, 128), FC)
        put(mm(tT[...], dus[:, cc]), UP_ROW + 3 * FC // 4 * n)

    red[0].send_row()
    transpose_into(tT, cs)
    put(mm(tT[...], dbs[...]), OUT_ROW)
    red[1].send_core()
    transpose_into(tT, h1s)

    def attention_back(p):
        sl = [slice(j * D + 128 * p, j * D + 128 * p + 128) for j in range(3)]

        @pl.loop(0, NI // 3)
        def _(c):
            rs = [pl.ds(pl.multiple_of((3 * c + m) * PAD, 16), PAD) for m in range(3)]
            q, k, v = ([qkv[r, t] for r in rs] for t in sl)
            dc = [dys[r, 128 * p:128 * p + 128] for r in rs]
            pr = [ps.at[(3 * c + m) * HEADS + 2 * p + h] for m in range(3) for h in range(2)]
            das = [mm_nt(dc[m // 2], half(v[m // 2], m % 2)) for m in range(6)]
            dss = []
            for m in range(6):
                prf = pr[m][...].astype(F32)
                t = prf * das[m]
                dss.append((t - prf * jnp.sum(t, axis=-1, keepdims=True)).astype(BF16))
            for m in range(3):
                a, b = 2 * m, 2 * m + 1
                dv = mm_tn(pr[a][...], half(dc[m], 0)) + mm_tn(pr[b][...], half(dc[m], 1))
                dq = mm(dss[a], half(k[m], 0)) + mm(dss[b], half(k[m], 1))
                dk = mm_tn(dss[a], half(q[m], 0)) + mm_tn(dss[b], half(q[m], 1))
                for j, o in enumerate((dq * 0.125, dk, dv)):
                    o = o.astype(BF16)
                    qkv[rs[m], sl[j]] = o
                    if j != 1:
                        gvec[6 + j:7 + j, 128 * p:128 * p + 128] += colsum(o.astype(F32))

    def qkv_grad(p):
        rhs = jnp.concatenate([qkv[:, j * D + 128 * p:j * D + 128 * p + 128] for j in range(3)], axis=1)
        put(mm(tT[...], rhs), QKV_ROW + 288 * p)

    attention_back(0)
    red[0].send_planes()
    red[1].send_row()
    qkv_grad(0)
    attention_back(1)
    red[0].send_back()
    qkv_grad(1)
    red[2].send_core()
    attention_back(2)
    red[1].send_planes()
    red[0].send_mate()
    red[2].send_row()
    qkv_grad(2)
    red[3].send_core()
    out_copy.wait()

    def first_norm_back(a, b):
        @pl.loop(a // CH4, b // CH4)
        def _(c):
            r = pl.ds(pl.multiple_of(c * (CH4 * PAD), 16), CH4 * PAD)
            dh = mm_nt(qkv[r, :], wqkv[...])
            xs = jnp.concatenate([padded(x_ref, c * CH4 + j, tmp) for j in range(CH4)], axis=0)
            n1, rs1 = norm_parts(xs)
            gvec[0:1, :] += colsum(dh * n1)
            gvec[1:2, :] += colsum(dh)
            ig = dbs[r, :].astype(F32) + norm_back(dh * vec(0), n1, rs1)
            for j in range(CH4):
                stage[c * CH4 + j] = ig[j * PAD:j * PAD + SEQ].astype(BF16)

    first_norm_back(0, 2)
    red[3].send_planes()
    red[1].send_back()
    first_norm_back(2, 6)
    red[2].send_planes()
    red[1].send_mate()
    first_norm_back(6, 10)
    red[3].send_row()
    red[2].send_back()
    first_norm_back(10, 12)

    ig_copy = pltpu.make_async_copy(stage, ig_ref, out_sem)
    ig_copy.start()
    for b in range(4):
        gvec[9 + b:10 + b, :] = gub[0:1, b * D:b * D + D]
    gv = gvec[...]
    for s in range(4):
        moved = gv if s == 0 else pltpu.roll(gv, D - 96 * s, 1)
        bias = gv if s % 2 == 0 else pltpu.roll(gv, D - 192, 1)
        br = 6 if s < 2 else 8
        tile = jnp.concatenate(
            [moved[0:6, 0:128], bias[br:br + 1, 0:128], bias[br:br + 1, 128:256]]
            + [gv[9 + s:10 + s, 128 * b:128 * b + 128] for b in range(3)] + [jnp.zeros((5, 128), F32)],
            axis=0,
        )
        gradv[s % 2, s // 2] = tile.astype(BF16)
    redv.send_core()
    red[3].send_back()
    red[2].send_mate()
    redv.send_planes()
    redv.send_row()
    for group in red:
        group.finish()
    redv.send_back()
    fin_copy = pltpu.make_async_copy(fin, fin_ref, out_sem2)
    fin_copy.start()
    finv_ref[...] = finv[...]
    for j in range(5):
        first[j].wait_send()
        second[j].wait_send()
        third[j].wait_send()
        if j != 1:
            mate[j].wait_send()
            fourth[j].wait_send()
    ig_copy.wait()
    fin_copy.wait()


def scratches():
    V = pltpu.VMEM
    bufs = []
    for _, m in SPREAD:
        bufs += [V((2, 32 * m, 128), BF16), V((3, 16 * m, 128), BF16), V((15, m, 128), BF16)]
    for n, full in ((32, 512), (16, 16)):
        bufs += [V((2, full, 128), BF16), V((15, 2, n, 128), BF16), V((2, n, 128), BF16), V((3, n, 128), BF16)]
    return [
        V((NI, SEQ, D), BF16), pltpu.SemaphoreType.DMA, pltpu.SemaphoreType.DMA,
        V((16, D), F32), V((16, D), BF16), V((PAD, D), F32), V((8, FF), F32), V((TROWS, D), BF16), V((D, TROWS), BF16), V((D, TROWS), BF16),
        V((TROWS, D), BF16), V((TROWS, 3 * D), BF16), V((NI * HEADS, PAD, PAD), BF16),
        V((TROWS, D), BF16), V((TROWS, D), BF16), V((TROWS, FF), BF16), V((TROWS, FF), BF16),
        V((TROWS, D), BF16),
        V((64, D), BF16), V((D, 3 * D), BF16), V((D, D), BF16), V((D, FF), BF16), V((FF, D), BF16),
        V((16, D), F32), V((16, D), F32), V((2, 2, GROWS, 128), BF16), V((2, 2, 16, 128), BF16),
        *bufs,
        V((GROWS, 128), BF16), V((16, 128), BF16),
        pltpu.SemaphoreType.DMA((200,)), pltpu.SemaphoreType.DMA((200,)),
    ]


def layer(x, dy, *params):
    S = jax.ShapeDtypeStruct
    vm, hbm = pl.BlockSpec(memory_space=pltpu.VMEM), pl.BlockSpec(memory_space=pl.ANY)
    return pl.pallas_call(
        body,
        out_shape=(S(x.shape, BF16), S(x.shape, BF16), S((GROWS, 128), BF16), S((16, 128), BF16)),
        in_specs=[vm, hbm] + [vm] * 12, out_specs=(hbm, hbm, hbm, vm),
        scratch_shapes=scratches(),
        compiler_params=pltpu.CompilerParams(
            vmem_limit_bytes=int(63.5 * 2**20), collective_id=0, has_side_effects=True),
    )(x, dy, *params)


def unpack_body(out_in, ig_in, fin, finv, out, ig, g1, s1, gqkv, gqv, go, bo, g2, s2, gup, bup, gd, bd, sems):
    copies = [pltpu.make_async_copy(out_in, out, sems.at[0]), pltpu.make_async_copy(ig_in, ig, sems.at[1])]
    for copy in copies:
        copy.start()
    for b in range(12):
        gup[:, 128 * b:128 * b + 128] = fin[UP_ROW + 96 * b:UP_ROW + 96 * b + 96, :].astype(F32)
    for b in range(3):
        gd[128 * b:128 * b + 128, :] = fin[DOWN_ROW + 384 * b:DOWN_ROW + 384 * b + 384, :].astype(F32).T
        go[:, 128 * b:128 * b + 128] = fin[OUT_ROW + 96 * b:OUT_ROW + 96 * b + 96, :].astype(F32)
    for p in range(3):
        for j in range(3):
            r = QKV_ROW + 288 * p + 96 * j
            gqkv[:, j * D + 128 * p:j * D + 128 * p + 128] = fin[r:r + 96, :].astype(F32)
    v = finv[...].astype(F32)
    for row, ref in enumerate((g1, s1, bo, g2, s2, bd)):
        ref[...] = v[row, 0:96]
    gqv[0:128] = v[6, :]
    gqv[128:192] = v[7, 0:64]
    for b in range(3):
        bup[128 * b:128 * b + 128] = v[8 + b, :]
    for copy in copies:
        copy.wait()


def unpack(outputs, input_grad, fin, finv):
    def S(*shape):
        return jax.ShapeDtypeStruct(shape, F32)

    vm, hbm = pl.BlockSpec(memory_space=pltpu.VMEM), pl.BlockSpec(memory_space=pl.ANY)
    whole = jax.ShapeDtypeStruct(outputs.shape, BF16)
    return pl.pallas_call(
        unpack_body,
        out_shape=(whole, whole, S(96), S(96), S(96, 3 * D), S(192), S(96, D), S(96), S(96), S(96),
                   S(96, FF), S(384), S(384, D), S(96)),
        in_specs=[hbm, hbm, vm, vm], out_specs=(hbm, hbm) + (vm,) * 12,
        scratch_shapes=[pltpu.SemaphoreType.DMA((2,))],
        compiler_params=pltpu.CompilerParams(vmem_limit_bytes=62 * 2**20),
    )(outputs, input_grad, fin, finv)


def local(*arrays):
    return unpack(*layer(*arrays))


def solution(mesh):
    tokens, whole, rows = P(("rep", "shard"), None, None), P("shard"), P("shard", None)
    vectors = (whole, whole, rows, whole, rows, whole, whole, whole, rows, whole, rows, whole)
    return jax.shard_map(
        local, mesh=mesh, in_specs=(tokens, tokens, *vectors),
        out_specs=(tokens, tokens, *vectors), check_vma=False)
```

```python
import math

import jax
import jax.numpy as jnp
from jax import lax
from jax.experimental import pallas as pl
from jax.experimental.pallas import tpu as pltpu
from jax.sharding import PartitionSpec as P

NI, SEQ, D, FF, HEADS = 12, 197, 384, 1536, 6
PAD = 208
ROWS = NI * PAD
TROWS = 2560
F32, BF16 = jnp.float32, jnp.bfloat16


def mm(a, b):
    return lax.dot_general(a, b, (((1,), (0,)), ((), ())), preferred_element_type=F32)


def mm_nt(a, b):
    return lax.dot_general(a, b, (((1,), (1,)), ((), ())), preferred_element_type=F32)


def mm_tn(a, b):
    return lax.dot_general(a, b, (((0,), (0,)), ((), ())), preferred_element_type=F32)


def norm_parts(v):
    avg = jnp.mean(v, axis=-1, keepdims=True)
    cen = v - avg
    var = jnp.mean(cen * cen, axis=-1, keepdims=True)
    rs = lax.rsqrt(var + 1e-6)
    return cen * rs, rs


def norm_back(e, n, rs):
    return rs * (e - jnp.mean(e, axis=-1, keepdims=True) - n * jnp.mean(e * n, axis=-1, keepdims=True))


def gelu_both(u):
    phi = 0.5 + 0.5 * lax.erf(u * math.sqrt(0.5))
    e = jnp.exp2(u * u * (-0.5 * math.log2(math.e)))
    return u * phi, phi + u * (e * (1.0 / math.sqrt(2 * math.pi)))


def colsum(v):
    return jnp.sum(v, axis=0, keepdims=True)

CH1, CH2, CH4, FC = 2, 2, 2, 512
MESH = pl.DeviceIdType.MESH

DOWN_ROW, UP_ROW, OUT_ROW, QKV_ROW = 0, 1152, 2304, 2592
GROWS = 3584
GROUPS = ((0, 64), (1024, 96), (2560, 32), (3072, 32))


class Comm:
    def __init__(self, ssem, rsem):
        self.ssem, self.rsem = ssem, rsem
        rep, shard = lax.axis_index("rep"), lax.axis_index("shard")
        self.z, self.y, self.lo = rep // 8, (rep // 2) % 4, rep % 2
        self.hi, self.core, self.plane = shard // 2, shard % 2, rep // 2
        self.sibling = (rep, self.hi * 2 + 1 - self.core)
        self.across = (self.plane * 2 + 1 - self.lo, (1 - self.hi) * 2 + self.core)
        self.row = []
        for dh, dl in ((0, 1), (1, 0), (1, 1)):
            ph, plo = (self.hi + dh) % 2, (self.lo + dl) % 2
            self.row.append(((self.plane * 2 + plo, ph * 2 + self.core), ph))
        self.planes = []
        for d in range(1, 16):
            pz, py = (self.z + d // 4) % 4, (self.y + d % 4) % 4
            q = pz * 4 + py
            self.planes.append(((q * 2 + self.lo, shard), q))

    def barrier(self, meanwhile):
        sem = pltpu.get_barrier_semaphore()
        peers = [self.sibling] + [d for d, _ in self.row] + [d for d, _ in self.planes]
        for dev in peers:
            pl.semaphore_signal(sem, inc=1, device_id=dev, device_id_type=MESH)
        meanwhile()
        pl.semaphore_wait(sem, len(peers))

    def copy(self, src, dst, slot, dev):
        return pltpu.make_async_remote_copy(
            src_ref=src, dst_ref=dst, send_sem=self.ssem.at[slot], recv_sem=self.rsem.at[slot],
            device_id=dev, device_id_type=MESH,
        )


class Reduce:
    def __init__(self, comm, base, grads, fin, start, n, rcore, rplane, part, rrow, scatter=True):
        c = comm
        self.c, self.n, self.scatter, self.start = c, n, scatter, start
        total = 16 * n if scatter else n
        self.grads, self.rcore, self.rplane, self.part, self.rrow, self.fin = (
            grads, rcore, rplane, part, rrow, fin)
        self.total = total
        rows = pl.ds(start, total)
        self.rows = rows
        self.core_copy = c.copy(grads.at[1 - c.core, :, rows, :], rcore, base, c.sibling)

        def piece(q):
            return pl.ds(pl.multiple_of(start + q * n, 16), n) if scatter else rows

        self.piece = piece
        self.plane_copies = [
            c.copy(grads.at[c.core, :, piece(q), :], rplane.at[d], base + 1 + d, dev)
            for d, (dev, q) in enumerate(c.planes)
        ]
        self.row_copies = [
            c.copy(part.at[h], rrow.at[d], base + 16 + d, dev)
            for d, (dev, h) in enumerate(c.row)
        ]
        if scatter:
            mine = piece(c.plane)
            self.back_copies = [
                c.copy(fin.at[mine, :], fin.at[mine, :], base + 19 + d, dev)
                for d, (dev, q) in enumerate(c.planes)
            ]

    def send_core(self):
        self.core_copy.start()

    def send_planes(self):
        self.core_copy.wait()
        step = 256 if self.total % 256 == 0 else 16

        @pl.loop(0, self.total // step)
        def _(b):
            off = pl.multiple_of(b * step, 16)
            r = pl.ds(pl.multiple_of(self.start + off, 16), step)
            for h in range(2):
                s = self.grads[self.c.core, h, r, :].astype(F32) + self.rcore[h, pl.ds(off, step), :].astype(F32)
                self.grads[self.c.core, h, r, :] = s.astype(BF16)

        for cp in self.plane_copies:
            cp.start()

    def send_row(self):
        for cp in self.plane_copies:
            cp.wait()
        for h in range(2):
            s = self.grads[self.c.core, h, self.piece(self.c.plane), :].astype(F32)
            for d in range(15):
                s = s + self.rplane[d, h].astype(F32)
            self.part[h] = s.astype(BF16)
        for cp in self.row_copies:
            cp.start()

    def send_back(self):
        for cp in self.row_copies:
            cp.wait()
        s = self.part[self.c.hi].astype(F32)
        for d in range(3):
            s = s + self.rrow[d].astype(F32)
        if self.scatter:
            self.fin[self.piece(self.c.plane), :] = s.astype(BF16)
            for cp in self.back_copies:
                cp.start()
        else:
            self.fin[...] = s.astype(BF16)

    def finish(self):
        for cp in self.back_copies:
            cp.wait()


def padded(ref, i, tmp):
    tmp[0:SEQ, :] = ref[i].astype(F32)
    return tmp[...]


def body(x_in, dy_ref, g1_in, s1_in, wqkv_in, qv_in, wo_in, bo_in, g2_in, s2_in, wup_in, bup_in,
         wd_in, bd_in,
         out_ref, ig_ref, fin_ref, finv_ref,
         x_ref, x_sem, stage, out_sem, packed, vin_ref, tmp, gub, dys, dyT, tT, h1s, qkv, ps, cs, h2s, gs, dus, dbs,
         vecs_all, wqkv, wo, wup, wd, vec_ref, gvec, grads, gradv,
         rcore0, rplane0, part0, rrow0, rcore1, rplane1, part1, rrow1,
         rcore2, rplane2, part2, rrow2, rcore3, rplane3, part3, rrow3, rcorev, rplanev, partv, rrowv, fin, finv, ssem, rsem):
    dy_copy = pltpu.make_async_copy(dy_ref, stage, out_sem)
    dy_copy.start()
    x_copy = pltpu.make_async_copy(x_in, x_ref, x_sem)
    x_copy.start()
    comm = Comm(ssem, rsem)
    shard = comm.hi * 2 + comm.core
    theirs = (1 - comm.hi) * 2 + comm.core

    def place(full, s):
        n = full.shape[0] // 4
        return full.at[pl.ds(pl.multiple_of(s * n, 16), n)]

    params = ((wqkv_in, wqkv), (vin_ref, vecs_all), (wo_in, wo), (wup_in, wup), (wd_in, wd))
    def meanwhile():
        packed[...] = jnp.zeros_like(packed)
        for row, ref in enumerate((g1_in, s1_in, bo_in, g2_in, s2_in, bd_in)):
            packed[row, 0:96] = ref[...].astype(F32)
        packed[6, 0:192] = qv_in[...].astype(F32)
        packed[7, :] = bup_in[...].astype(F32)
        row = lax.broadcasted_iota(jnp.int32, (16, 1), 0)
        own = packed[...]
        six = jnp.where(row < 6, pltpu.roll(own, 96 * shard, 1), 0.0)
        two = pltpu.roll(own, 192 * comm.core, 1)[6:7, :]
        two = jnp.where(row == 6 + 2 * comm.hi, two, 0.0)
        up = jnp.where(row == 9 + shard, own[7:8, :], 0.0)
        vin_ref[...] = (six + two + up).astype(BF16)
        for own, full in params:
            n = own.shape[0]
            full[pl.ds(pl.multiple_of(shard * n, 16), n), :] = own[...]
        tmp[...] = jnp.zeros_like(tmp)
        gvec[...] = jnp.zeros_like(gvec)
        gub[...] = jnp.zeros_like(gub)
        for t in (dys, h1s, cs, h2s, gs, dus, dbs, qkv):
            t[ROWS:TROWS, :] = jnp.zeros((TROWS - ROWS, t.shape[1]), t.dtype)
        grads[:, :, QKV_ROW + 864:, :] = jnp.zeros((2, 2, GROWS - QKV_ROW - 864, 128), BF16)
        dy_copy.wait()

        @pl.loop(0, NI)
        def _(i):
            r = pl.ds(pl.multiple_of(i * PAD, 16), PAD)
            dy = padded(stage, i, tmp)
            dys[r, :] = dy.astype(BF16)
            gvec[5:6, :] += colsum(dy)

    comm.barrier(meanwhile)
    first, second, third = [], [], []
    for j, (own, full) in enumerate(params):
        first.append(comm.copy(own, place(full, shard), 3 * j, comm.across))
        second.append(comm.copy(own, place(full, shard), 3 * j + 1, comm.sibling))
        third.append(comm.copy(place(full, theirs), place(full, theirs), 3 * j + 2, comm.sibling))

    def send(j):
        first[j].start()
        second[j].start()

    send(1)
    send(0)

    def forward(j):
        first[j].wait_recv()
        third[j].start()

    def gathered(j):
        second[j].wait_recv()
        third[j].wait_recv()

    red = [Reduce(comm, 16 + 40 * g, grads, fin, start, n, *bufs)
           for g, ((start, n), bufs) in enumerate(zip(GROUPS, (
               (rcore0, rplane0, part0, rrow0), (rcore1, rplane1, part1, rrow1),
               (rcore2, rplane2, part2, rrow2), (rcore3, rplane3, part3, rrow3))))]
    redv = Reduce(comm, 176, gradv, finv, 0, 16, rcorev, rplanev, partv, rrowv, scatter=False)

    def vec(r):
        return vec_ref[r:r + 1, :]

    def vcat(r, n):
        return jnp.concatenate([vec_ref[r + j:r + j + 1, :] for j in range(n)], axis=1)

    def transpose_into(dst, src):
        @pl.loop(0, TROWS // 256)
        def _(b):
            r = pl.ds(pl.multiple_of(b * 256, 256), 256)
            dst[:, r] = src[r, :].T

    transpose_into(dyT, dys)
    forward(1)
    gathered(1)
    vec_ref[...] = (
        vecs_all[0:16, :].astype(F32) + vecs_all[16:32, :].astype(F32)
        + vecs_all[32:48, :].astype(F32) + vecs_all[48:64, :].astype(F32)
    )

    def first_norm(a, b):
        @pl.loop(a, b)
        def _(i):
            r = pl.ds(pl.multiple_of(i * PAD, 16), PAD)
            n, _ = norm_parts(padded(x_ref, i, tmp))
            h1s[r, :] = (n * vec(0) + vec(1)).astype(BF16)

    x_copy.wait()
    first_norm(0, 9)
    forward(0)
    for j in (2, 3, 4):
        send(j)
    first_norm(9, 12)
    gathered(0)

    lane = lax.broadcasted_iota(jnp.int32, (1, 128), 1)
    halves = (lane < 64, lane >= 64)
    lastcol = lax.broadcasted_iota(jnp.int32, (1, PAD - 128), 1) < SEQ - 128
    zero = jnp.zeros((), BF16)

    def half(v, h):
        return jnp.where(halves[h], v, zero)

    @pl.loop(0, NI // CH1)
    def _(c):
        r = pl.ds(pl.multiple_of(c * (CH1 * PAD), 16), CH1 * PAD)
        p = mm(h1s[r, :], wqkv[...]) + vcat(6, 3)
        qkv[r, 0:D] = (p[:, 0:D] * 0.125).astype(BF16)
        qkv[r, D:3 * D] = p[:, D:].astype(BF16)

    def attention(first_image, last_image):
        @pl.loop(first_image, last_image)
        def _(i):
            r = pl.ds(pl.multiple_of(i * PAD, 16), PAD)
            q, k, v = ([qkv[r, j * D + 128 * p:j * D + 128 * p + 128] for p in range(3)] for j in range(3))
            ss = [mm_nt(q[h // 2], half(k[h // 2], h % 2)) for h in range(6)]
            pr = []
            for h in range(6):
                s = jnp.concatenate([ss[h][:, 0:128], jnp.where(lastcol, ss[h][:, 128:PAD], -1e30)], axis=1)
                e = jnp.exp(s - jnp.max(s, axis=-1, keepdims=True))
                pr.append((e * (1.0 / jnp.sum(e, axis=-1, keepdims=True))).astype(BF16))
                ps[i * HEADS + h] = pr[h]
            for p in range(3):
                acc = mm(pr[2 * p], half(v[p], 0)) + mm(pr[2 * p + 1], half(v[p], 1))
                cs[r, 128 * p:128 * p + 128] = acc.astype(BF16)

    attention(0, 9)
    forward(2)
    forward(3)
    attention(9, 12)
    forward(4)
    for j in (2, 3, 4):
        gathered(j)

    @pl.loop(0, NI // CH2)
    def _(c):
        r = pl.ds(pl.multiple_of(c * (CH2 * PAD), 16), CH2 * PAD)
        xs = jnp.concatenate([padded(x_ref, c * CH2 + j, tmp) for j in range(CH2)], axis=0)
        x1 = xs + mm(cs[r, :], wo[...]) + vec(2)
        n2, rs2 = norm_parts(x1)
        h2 = (n2 * vec(3) + vec(4)).astype(BF16)
        h2s[r, :] = h2
        dy = dys[r, :]
        bup = vcat(9, 4)
        acc, dh = x1 + vec(5), None
        for f in range(FF // FC):
            fc = slice(f * FC, f * FC + FC)
            u = mm(h2, wup[:, fc]) + bup[:, fc]
            g, gp = gelu_both(u)
            g = g.astype(BF16)
            gs[r, fc] = g
            acc = acc + mm(g, wd[fc, :])
            du = (mm_nt(dy, wd[fc, :]) * gp).astype(BF16)
            dus[r, fc] = du
            gub[0:1, fc] += colsum(du.astype(F32))
            o = mm_nt(du, wup[:, fc])
            dh = o if dh is None else dh + o
        for j in range(CH2):
            stage[c * CH2 + j] = acc[j * PAD:j * PAD + SEQ].astype(BF16)
        gvec[3:4, :] += colsum(dh * n2)
        gvec[4:5, :] += colsum(dh)
        dx1 = dy.astype(F32) + norm_back(dh * vec(3), n2, rs2)
        db = dx1.astype(BF16)
        dbs[r, :] = db
        gvec[2:3, :] += colsum(db.astype(F32))
        dys[r, :] = mm_nt(db, wo[...]).astype(BF16)

    out_copy = pltpu.make_async_copy(stage, out_ref, out_sem)
    out_copy.start()

    def put(value, row):
        value = value.astype(BF16)
        for s in range(4):
            for b in range(value.shape[1] // 128):
                r = pl.ds(pl.multiple_of(row + 96 * b, 16), 96)
                grads[s % 2, s // 2, r, :] = value[96 * s:96 * s + 96, 128 * b:128 * b + 128]

    @pl.loop(0, 2)
    def _(h):
        for core in range(2):
            cc = pl.ds(pl.multiple_of(h * 768 + core * 384, 128), 384)
            value = mm(dyT[...], gs[:, cc]).astype(BF16)
            for b in range(3):
                grads[core, h, DOWN_ROW + 384 * b:DOWN_ROW + 384 * b + 384, :] = value[:, 128 * b:128 * b + 128]

    red[0].send_core()
    transpose_into(tT, h2s)

    @pl.loop(0, FF // FC)
    def _(n):
        cc = pl.ds(pl.multiple_of(n * FC, 128), FC)
        put(mm(tT[...], dus[:, cc]), UP_ROW + 3 * FC // 4 * n)

    red[0].send_planes()

    transpose_into(tT, cs)
    put(mm(tT[...], dbs[...]), OUT_ROW)
    red[1].send_core()
    transpose_into(tT, h1s)

    def attention_back(p):
        sl = [slice(j * D + 128 * p, j * D + 128 * p + 128) for j in range(3)]

        @pl.loop(0, NI // 3)
        def _(c):
            rs = [pl.ds(pl.multiple_of((3 * c + m) * PAD, 16), PAD) for m in range(3)]
            q, k, v = ([qkv[r, t] for r in rs] for t in sl)
            dc = [dys[r, 128 * p:128 * p + 128] for r in rs]
            pr = [ps.at[(3 * c + m) * HEADS + 2 * p + h] for m in range(3) for h in range(2)]
            das = [mm_nt(dc[m // 2], half(v[m // 2], m % 2)) for m in range(6)]
            dss = []
            for m in range(6):
                prf = pr[m][...].astype(F32)
                t = prf * das[m]
                dss.append((t - prf * jnp.sum(t, axis=-1, keepdims=True)).astype(BF16))
            for m in range(3):
                a, b = 2 * m, 2 * m + 1
                dv = mm_tn(pr[a][...], half(dc[m], 0)) + mm_tn(pr[b][...], half(dc[m], 1))
                dq = mm(dss[a], half(k[m], 0)) + mm(dss[b], half(k[m], 1))
                dk = mm_tn(dss[a], half(q[m], 0)) + mm_tn(dss[b], half(q[m], 1))
                for j, o in enumerate((dq * 0.125, dk, dv)):
                    o = o.astype(BF16)
                    qkv[rs[m], sl[j]] = o
                    if j != 1:
                        gvec[6 + j:7 + j, 128 * p:128 * p + 128] += colsum(o.astype(F32))

    def qkv_grad(p):
        rhs = jnp.concatenate([qkv[:, j * D + 128 * p:j * D + 128 * p + 128] for j in range(3)], axis=1)
        put(mm(tT[...], rhs), QKV_ROW + 288 * p)

    attention_back(0)
    red[1].send_planes()
    qkv_grad(0)
    attention_back(1)
    red[0].send_row()
    qkv_grad(1)
    red[2].send_core()
    attention_back(2)
    red[0].send_back()
    red[2].send_planes()
    qkv_grad(2)
    red[3].send_core()
    red[1].send_row()
    out_copy.wait()

    def first_norm_back(a, b):
        @pl.loop(a // CH4, b // CH4)
        def _(c):
            r = pl.ds(pl.multiple_of(c * (CH4 * PAD), 16), CH4 * PAD)
            dh = mm_nt(qkv[r, :], wqkv[...])
            xs = jnp.concatenate([padded(x_ref, c * CH4 + j, tmp) for j in range(CH4)], axis=0)
            n1, rs1 = norm_parts(xs)
            gvec[0:1, :] += colsum(dh * n1)
            gvec[1:2, :] += colsum(dh)
            ig = dbs[r, :].astype(F32) + norm_back(dh * vec(0), n1, rs1)
            for j in range(CH4):
                stage[c * CH4 + j] = ig[j * PAD:j * PAD + SEQ].astype(BF16)

    first_norm_back(0, 4)
    red[3].send_planes()
    first_norm_back(4, 8)
    red[1].send_back()
    red[2].send_row()
    first_norm_back(8, 12)

    ig_copy = pltpu.make_async_copy(stage, ig_ref, out_sem)
    ig_copy.start()
    for b in range(4):
        gvec[9 + b:10 + b, :] = gub[0:1, b * D:b * D + D]
    gv = gvec[...]
    for s in range(4):
        moved = gv if s == 0 else pltpu.roll(gv, D - 96 * s, 1)
        bias = gv if s % 2 == 0 else pltpu.roll(gv, D - 192, 1)
        br = 6 if s < 2 else 8
        tile = jnp.concatenate(
            [moved[0:6, 0:128], bias[br:br + 1, 0:128], bias[br:br + 1, 128:256]]
            + [gv[9 + s:10 + s, 128 * b:128 * b + 128] for b in range(3)] + [jnp.zeros((5, 128), F32)],
            axis=0,
        )
        gradv[s % 2, s // 2] = tile.astype(BF16)
    redv.send_core()
    red[3].send_row()
    redv.send_planes()
    red[2].send_back()
    red[3].send_back()
    redv.send_row()
    for g in range(4):
        red[g].finish()
    redv.send_back()
    fin_copy = pltpu.make_async_copy(fin, fin_ref, x_sem)
    fin_copy.start()
    finv_ref[...] = finv[...]
    for j in range(5):
        first[j].wait_send()
        second[j].wait_send()
        third[j].wait_send()
    ig_copy.wait()
    fin_copy.wait()


def scratches():
    V = pltpu.VMEM
    bufs = []
    for n, full in ((64, 1024), (96, 1536), (32, 512), (32, 512), (16, 16)):
        bufs += [V((2, full, 128), BF16), V((15, 2, n, 128), BF16), V((2, n, 128), BF16), V((3, n, 128), BF16)]
    return [
        V((NI, SEQ, D), BF16), pltpu.SemaphoreType.DMA, V((NI, SEQ, D), BF16), pltpu.SemaphoreType.DMA,
        V((16, D), F32), V((16, D), BF16), V((PAD, D), F32), V((8, FF), F32), V((TROWS, D), BF16), V((D, TROWS), BF16), V((D, TROWS), BF16),
        V((TROWS, D), BF16), V((TROWS, 3 * D), BF16), V((NI * HEADS, PAD, PAD), BF16),
        V((TROWS, D), BF16), V((TROWS, D), BF16), V((TROWS, FF), BF16), V((TROWS, FF), BF16),
        V((TROWS, D), BF16),
        V((64, D), BF16), V((D, 3 * D), BF16), V((D, D), BF16), V((D, FF), BF16), V((FF, D), BF16),
        V((16, D), F32), V((16, D), F32), V((2, 2, GROWS, 128), BF16), V((2, 2, 16, 128), BF16),
        *bufs,
        V((GROWS, 128), BF16), V((16, 128), BF16),
        pltpu.SemaphoreType.DMA((200,)), pltpu.SemaphoreType.DMA((200,)),
    ]


def layer(x, dy, *params):
    S = jax.ShapeDtypeStruct
    vm, hbm = pl.BlockSpec(memory_space=pltpu.VMEM), pl.BlockSpec(memory_space=pl.ANY)
    return pl.pallas_call(
        body,
        out_shape=(S(x.shape, BF16), S(x.shape, BF16), S((GROWS, 128), BF16), S((16, 128), BF16)),
        in_specs=[hbm, hbm] + [vm] * 12, out_specs=(hbm, hbm, hbm, vm),
        scratch_shapes=scratches(),
        compiler_params=pltpu.CompilerParams(
            vmem_limit_bytes=int(63.5 * 2**20), collective_id=0, has_side_effects=True),
    )(x, dy, *params)


def unpack_body(out_in, ig_in, fin, finv, out, ig, g1, s1, gqkv, gqv, go, bo, g2, s2, gup, bup, gd, bd, held, sems):
    pairs = ((out_in, out), (ig_in, ig))
    reads, copies = [], []
    for j, (src, dst) in enumerate(pairs):
        for p in range(4):
            some = pl.ds(3 * p, 3)
            reads.append(pltpu.make_async_copy(src.at[some], held.at[j, some], sems.at[0, 4 * j + p]))
            copies.append(pltpu.make_async_copy(held.at[j, some], dst.at[some], sems.at[1, 4 * j + p]))
    for read in reads:
        read.start()
    for read, copy in zip(reads, copies):
        read.wait()
        copy.start()
    for b in range(12):
        gup[:, 128 * b:128 * b + 128] = fin[UP_ROW + 96 * b:UP_ROW + 96 * b + 96, :].astype(F32)
    for b in range(3):
        gd[128 * b:128 * b + 128, :] = fin[DOWN_ROW + 384 * b:DOWN_ROW + 384 * b + 384, :].astype(F32).T
        go[:, 128 * b:128 * b + 128] = fin[OUT_ROW + 96 * b:OUT_ROW + 96 * b + 96, :].astype(F32)
    for p in range(3):
        for j in range(3):
            r = QKV_ROW + 288 * p + 96 * j
            gqkv[:, j * D + 128 * p:j * D + 128 * p + 128] = fin[r:r + 96, :].astype(F32)
    v = finv[...].astype(F32)
    for row, ref in enumerate((g1, s1, bo, g2, s2, bd)):
        ref[...] = v[row, 0:96]
    gqv[0:128] = v[6, :]
    gqv[128:192] = v[7, 0:64]
    for b in range(3):
        bup[128 * b:128 * b + 128] = v[8 + b, :]
    for copy in copies:
        copy.wait()


def unpack(outputs, input_grad, fin, finv):
    def S(*shape):
        return jax.ShapeDtypeStruct(shape, F32)

    vm, hbm = pl.BlockSpec(memory_space=pltpu.VMEM), pl.BlockSpec(memory_space=pl.ANY)
    whole = jax.ShapeDtypeStruct(outputs.shape, BF16)
    return pl.pallas_call(
        unpack_body,
        out_shape=(whole, whole, S(96), S(96), S(96, 3 * D), S(192), S(96, D), S(96), S(96), S(96),
                   S(96, FF), S(384), S(384, D), S(96)),
        in_specs=[hbm, hbm, vm, vm], out_specs=(hbm, hbm) + (vm,) * 12,
        scratch_shapes=[pltpu.VMEM((2, *outputs.shape), BF16), pltpu.SemaphoreType.DMA((2, 8))],
        compiler_params=pltpu.CompilerParams(vmem_limit_bytes=62 * 2**20),
    )(outputs, input_grad, fin, finv)


def local(*arrays):
    return unpack(*layer(*arrays))


def solution(mesh):
    tokens, whole, rows = P(("rep", "shard"), None, None), P("shard"), P("shard", None)
    vectors = (whole, whole, rows, whole, rows, whole, whole, whole, rows, whole, rows, whole)
    return jax.shard_map(
        local, mesh=mesh, in_specs=(tokens, tokens, *vectors),
        out_specs=(tokens, tokens, *vectors), check_vma=False)
```

```python
import math

import jax
import jax.numpy as jnp
from jax import lax
from jax.experimental import pallas as pl
from jax.experimental.pallas import tpu as pltpu
from jax.sharding import PartitionSpec as P

NI, SEQ, D, FF, HEADS = 12, 197, 384, 1536, 6
PAD = 208
ROWS = NI * PAD
TROWS = 2560
F32, BF16 = jnp.float32, jnp.bfloat16


def mm(a, b):
    return lax.dot_general(a, b, (((1,), (0,)), ((), ())), preferred_element_type=F32)


def mm_nt(a, b):
    return lax.dot_general(a, b, (((1,), (1,)), ((), ())), preferred_element_type=F32)


def mm_tn(a, b):
    return lax.dot_general(a, b, (((0,), (0,)), ((), ())), preferred_element_type=F32)


def norm_parts(v):
    avg = jnp.mean(v, axis=-1, keepdims=True)
    cen = v - avg
    var = jnp.mean(cen * cen, axis=-1, keepdims=True)
    rs = lax.rsqrt(var + 1e-6)
    return cen * rs, rs


def norm_back(e, n, rs):
    return rs * (e - jnp.mean(e, axis=-1, keepdims=True) - n * jnp.mean(e * n, axis=-1, keepdims=True))


def gelu_both(u):
    phi = 0.5 + 0.5 * lax.erf(u * math.sqrt(0.5))
    e = jnp.exp2(u * u * (-0.5 * math.log2(math.e)))
    return u * phi, phi + u * (e * (1.0 / math.sqrt(2 * math.pi)))


def colsum(v):
    return jnp.sum(v, axis=0, keepdims=True)

CH1, CH2, CH4, FC = 2, 2, 2, 512
MESH = pl.DeviceIdType.MESH

DOWN_ROW, UP_ROW, OUT_ROW, QKV_ROW = 0, 1152, 2304, 2592
GROWS = 3584
GROUPS = ((0, 64), (1024, 96), (2560, 32), (3072, 32))


class Comm:
    def __init__(self, ssem, rsem):
        self.ssem, self.rsem = ssem, rsem
        rep, shard = lax.axis_index("rep"), lax.axis_index("shard")
        self.z, self.y, self.lo = rep // 8, (rep // 2) % 4, rep % 2
        self.hi, self.core, self.plane = shard // 2, shard % 2, rep // 2
        self.sibling = (rep, self.hi * 2 + 1 - self.core)
        self.across = (self.plane * 2 + 1 - self.lo, (1 - self.hi) * 2 + self.core)
        self.row = []
        for dh, dl in ((0, 1), (1, 0), (1, 1)):
            ph, plo = (self.hi + dh) % 2, (self.lo + dl) % 2
            self.row.append(((self.plane * 2 + plo, ph * 2 + self.core), ph))
        self.planes = []
        for d in range(1, 16):
            pz, py = (self.z + d // 4) % 4, (self.y + d % 4) % 4
            q = pz * 4 + py
            self.planes.append(((q * 2 + self.lo, shard), q))

    def barrier(self, meanwhile):
        sem = pltpu.get_barrier_semaphore()
        peers = [self.sibling] + [d for d, _ in self.row] + [d for d, _ in self.planes]
        for dev in peers:
            pl.semaphore_signal(sem, inc=1, device_id=dev, device_id_type=MESH)
        meanwhile()
        pl.semaphore_wait(sem, len(peers))

    def copy(self, src, dst, slot, dev):
        return pltpu.make_async_remote_copy(
            src_ref=src, dst_ref=dst, send_sem=self.ssem.at[slot], recv_sem=self.rsem.at[slot],
            device_id=dev, device_id_type=MESH,
        )


class Reduce:
    def __init__(self, comm, base, grads, fin, start, n, rcore, rplane, part, rrow, scatter=True):
        c = comm
        self.c, self.n, self.scatter, self.start = c, n, scatter, start
        total = 16 * n if scatter else n
        self.grads, self.rcore, self.rplane, self.part, self.rrow, self.fin = (
            grads, rcore, rplane, part, rrow, fin)
        self.total = total
        rows = pl.ds(start, total)
        self.rows = rows
        self.core_copy = c.copy(grads.at[1 - c.core, :, rows, :], rcore, base, c.sibling)

        def piece(q):
            return pl.ds(pl.multiple_of(start + q * n, 16), n) if scatter else rows

        self.piece = piece
        self.plane_copies = [
            c.copy(grads.at[c.core, :, piece(q), :], rplane.at[d], base + 1 + d, dev)
            for d, (dev, q) in enumerate(c.planes)
        ]
        self.row_copies = [
            c.copy(part.at[h], rrow.at[d], base + 16 + d, dev)
            for d, (dev, h) in enumerate(c.row)
        ]
        if scatter:
            mine = piece(c.plane)
            self.back_copies = [
                c.copy(fin.at[mine, :], fin.at[mine, :], base + 19 + d, dev)
                for d, (dev, q) in enumerate(c.planes)
            ]

    def send_core(self):
        self.core_copy.start()

    def send_planes(self):
        self.core_copy.wait()
        step = 256 if self.total % 256 == 0 else 16

        @pl.loop(0, self.total // step)
        def _(b):
            off = pl.multiple_of(b * step, 16)
            r = pl.ds(pl.multiple_of(self.start + off, 16), step)
            for h in range(2):
                s = self.grads[self.c.core, h, r, :].astype(F32) + self.rcore[h, pl.ds(off, step), :].astype(F32)
                self.grads[self.c.core, h, r, :] = s.astype(BF16)

        for cp in self.plane_copies:
            cp.start()

    def send_row(self):
        for cp in self.plane_copies:
            cp.wait()
        for h in range(2):
            s = self.grads[self.c.core, h, self.piece(self.c.plane), :].astype(F32)
            for d in range(15):
                s = s + self.rplane[d, h].astype(F32)
            self.part[h] = s.astype(BF16)
        for cp in self.row_copies:
            cp.start()

    def send_back(self):
        for cp in self.row_copies:
            cp.wait()
        s = self.part[self.c.hi].astype(F32)
        for d in range(3):
            s = s + self.rrow[d].astype(F32)
        if self.scatter:
            self.fin[self.piece(self.c.plane), :] = s.astype(BF16)
            for cp in self.back_copies:
                cp.start()
        else:
            self.fin[...] = s.astype(BF16)

    def finish(self):
        for cp in self.back_copies:
            cp.wait()


def padded(ref, i, tmp):
    tmp[0:SEQ, :] = ref[i].astype(F32)
    return tmp[...]


def body(x_in, dy_ref, g1_in, s1_in, wqkv_in, qv_in, wo_in, bo_in, g2_in, s2_in, wup_in, bup_in,
         wd_in, bd_in,
         out_ref, ig_ref, fin_ref, finv_ref,
         x_ref, x_sem, stage, out_sem, packed, vin_ref, tmp, gub, dys, dyT, tT, h1s, qkv, ps, cs, h2s, gs, dus, dbs,
         vecs_all, wqkv, wo, wup, wd, vec_ref, gvec, grads, gradv,
         rcore0, rplane0, part0, rrow0, rcore1, rplane1, part1, rrow1,
         rcore2, rplane2, part2, rrow2, rcore3, rplane3, part3, rrow3, rcorev, rplanev, partv, rrowv, fin, finv, ssem, rsem):
    dy_copy = pltpu.make_async_copy(dy_ref, stage, out_sem)
    dy_copy.start()
    x_copy = pltpu.make_async_copy(x_in, x_ref, x_sem)
    x_copy.start()
    comm = Comm(ssem, rsem)
    shard = comm.hi * 2 + comm.core
    theirs = (1 - comm.hi) * 2 + comm.core

    def place(full, s):
        n = full.shape[0] // 4
        return full.at[pl.ds(pl.multiple_of(s * n, 16), n)]

    params = ((wqkv_in, wqkv), (vin_ref, vecs_all), (wo_in, wo), (wup_in, wup), (wd_in, wd))
    def meanwhile():
        packed[...] = jnp.zeros_like(packed)
        for row, ref in enumerate((g1_in, s1_in, bo_in, g2_in, s2_in, bd_in)):
            packed[row, 0:96] = ref[...].astype(F32)
        packed[6, 0:192] = qv_in[...].astype(F32)
        packed[7, :] = bup_in[...].astype(F32)
        row = lax.broadcasted_iota(jnp.int32, (16, 1), 0)
        own = packed[...]
        six = jnp.where(row < 6, pltpu.roll(own, 96 * shard, 1), 0.0)
        two = pltpu.roll(own, 192 * comm.core, 1)[6:7, :]
        two = jnp.where(row == 6 + 2 * comm.hi, two, 0.0)
        up = jnp.where(row == 9 + shard, own[7:8, :], 0.0)
        vin_ref[...] = (six + two + up).astype(BF16)
        for own, full in params:
            n = own.shape[0]
            full[pl.ds(pl.multiple_of(shard * n, 16), n), :] = own[...]
        tmp[...] = jnp.zeros_like(tmp)
        gvec[...] = jnp.zeros_like(gvec)
        gub[...] = jnp.zeros_like(gub)
        for t in (dys, h1s, cs, h2s, gs, dus, dbs, qkv):
            t[ROWS:TROWS, :] = jnp.zeros((TROWS - ROWS, t.shape[1]), t.dtype)
        grads[:, :, QKV_ROW + 864:, :] = jnp.zeros((2, 2, GROWS - QKV_ROW - 864, 128), BF16)
        dy_copy.wait()

        @pl.loop(0, NI)
        def _(i):
            r = pl.ds(pl.multiple_of(i * PAD, 16), PAD)
            dy = padded(stage, i, tmp)
            dys[r, :] = dy.astype(BF16)
            gvec[5:6, :] += colsum(dy)

    comm.barrier(meanwhile)
    first, second, third = [], [], []
    for j, (own, full) in enumerate(params):
        first.append(comm.copy(own, place(full, shard), 3 * j, comm.across))
        second.append(comm.copy(own, place(full, shard), 3 * j + 1, comm.sibling))
        third.append(comm.copy(place(full, theirs), place(full, theirs), 3 * j + 2, comm.sibling))

    def send(j):
        first[j].start()
        second[j].start()

    send(1)
    send(0)

    def forward(j):
        first[j].wait_recv()
        third[j].start()

    def gathered(j):
        second[j].wait_recv()
        third[j].wait_recv()

    red = [Reduce(comm, 16 + 40 * g, grads, fin, start, n, *bufs)
           for g, ((start, n), bufs) in enumerate(zip(GROUPS, (
               (rcore0, rplane0, part0, rrow0), (rcore1, rplane1, part1, rrow1),
               (rcore2, rplane2, part2, rrow2), (rcore3, rplane3, part3, rrow3))))]
    redv = Reduce(comm, 176, gradv, finv, 0, 16, rcorev, rplanev, partv, rrowv, scatter=False)

    def vec(r):
        return vec_ref[r:r + 1, :]

    def vcat(r, n):
        return jnp.concatenate([vec_ref[r + j:r + j + 1, :] for j in range(n)], axis=1)

    def transpose_into(dst, src):
        @pl.loop(0, TROWS // 256)
        def _(b):
            r = pl.ds(pl.multiple_of(b * 256, 256), 256)
            dst[:, r] = src[r, :].T

    transpose_into(dyT, dys)
    forward(1)
    gathered(1)
    vec_ref[...] = (
        vecs_all[0:16, :].astype(F32) + vecs_all[16:32, :].astype(F32)
        + vecs_all[32:48, :].astype(F32) + vecs_all[48:64, :].astype(F32)
    )

    def first_norm(a, b):
        @pl.loop(a, b)
        def _(i):
            r = pl.ds(pl.multiple_of(i * PAD, 16), PAD)
            n, _ = norm_parts(padded(x_ref, i, tmp))
            h1s[r, :] = (n * vec(0) + vec(1)).astype(BF16)

    x_copy.wait()
    first_norm(0, 9)
    forward(0)
    for j in (2, 3, 4):
        send(j)
    first_norm(9, 12)
    gathered(0)

    lane = lax.broadcasted_iota(jnp.int32, (1, 128), 1)
    halves = (lane < 64, lane >= 64)
    lastcol = lax.broadcasted_iota(jnp.int32, (1, PAD - 128), 1) < SEQ - 128
    zero = jnp.zeros((), BF16)

    def half(v, h):
        return jnp.where(halves[h], v, zero)

    @pl.loop(0, NI // CH1)
    def _(c):
        r = pl.ds(pl.multiple_of(c * (CH1 * PAD), 16), CH1 * PAD)
        p = mm(h1s[r, :], wqkv[...]) + vcat(6, 3)
        qkv[r, 0:D] = (p[:, 0:D] * 0.125).astype(BF16)
        qkv[r, D:3 * D] = p[:, D:].astype(BF16)

    def attention(first_image, last_image):
        @pl.loop(first_image, last_image)
        def _(i):
            r = pl.ds(pl.multiple_of(i * PAD, 16), PAD)
            q, k, v = ([qkv[r, j * D + 128 * p:j * D + 128 * p + 128] for p in range(3)] for j in range(3))
            ss = [mm_nt(q[h // 2], half(k[h // 2], h % 2)) for h in range(6)]
            pr = []
            for h in range(6):
                s = jnp.concatenate([ss[h][:, 0:128], jnp.where(lastcol, ss[h][:, 128:PAD], -1e30)], axis=1)
                e = jnp.exp(s - jnp.max(s, axis=-1, keepdims=True))
                pr.append((e * (1.0 / jnp.sum(e, axis=-1, keepdims=True))).astype(BF16))
                ps[i * HEADS + h] = pr[h]
            for p in range(3):
                acc = mm(pr[2 * p], half(v[p], 0)) + mm(pr[2 * p + 1], half(v[p], 1))
                cs[r, 128 * p:128 * p + 128] = acc.astype(BF16)

    attention(0, 9)
    forward(2)
    forward(3)
    attention(9, 12)
    forward(4)
    for j in (2, 3, 4):
        gathered(j)

    @pl.loop(0, NI // CH2)
    def _(c):
        r = pl.ds(pl.multiple_of(c * (CH2 * PAD), 16), CH2 * PAD)
        xs = jnp.concatenate([padded(x_ref, c * CH2 + j, tmp) for j in range(CH2)], axis=0)
        x1 = xs + mm(cs[r, :], wo[...]) + vec(2)
        n2, rs2 = norm_parts(x1)
        h2 = (n2 * vec(3) + vec(4)).astype(BF16)
        h2s[r, :] = h2
        dy = dys[r, :]
        bup = vcat(9, 4)
        for f in range(FF // FC):
            fc = slice(f * FC, f * FC + FC)
            u = mm(h2, wup[:, fc]) + bup[:, fc]
            da = mm_nt(dy, wd[fc, :])
            g, gp = gelu_both(u)
            gs[r, fc] = g.astype(BF16)
            du = (da * gp).astype(BF16)
            dus[r, fc] = du
            gub[0:1, fc] += colsum(du.astype(F32))
        acc = x1 + vec(5) + mm(gs[r, :], wd[...])
        dh = mm_nt(dus[r, :], wup[...])
        for j in range(CH2):
            stage[c * CH2 + j] = acc[j * PAD:j * PAD + SEQ].astype(BF16)
        gvec[3:4, :] += colsum(dh * n2)
        gvec[4:5, :] += colsum(dh)
        dx1 = dy.astype(F32) + norm_back(dh * vec(3), n2, rs2)
        db = dx1.astype(BF16)
        dbs[r, :] = db
        gvec[2:3, :] += colsum(db.astype(F32))
        dys[r, :] = mm_nt(db, wo[...]).astype(BF16)

    out_copy = pltpu.make_async_copy(stage, out_ref, out_sem)
    out_copy.start()

    def put(value, row):
        value = value.astype(BF16)
        for s in range(4):
            for b in range(value.shape[1] // 128):
                r = pl.ds(pl.multiple_of(row + 96 * b, 16), 96)
                grads[s % 2, s // 2, r, :] = value[96 * s:96 * s + 96, 128 * b:128 * b + 128]

    @pl.loop(0, 2)
    def _(h):
        for core in range(2):
            cc = pl.ds(pl.multiple_of(h * 768 + core * 384, 128), 384)
            value = mm(dyT[...], gs[:, cc]).astype(BF16)
            for b in range(3):
                grads[core, h, DOWN_ROW + 384 * b:DOWN_ROW + 384 * b + 384, :] = value[:, 128 * b:128 * b + 128]

    red[0].send_core()
    transpose_into(tT, h2s)

    @pl.loop(0, FF // FC)
    def _(n):
        cc = pl.ds(pl.multiple_of(n * FC, 128), FC)
        put(mm(tT[...], dus[:, cc]), UP_ROW + 3 * FC // 4 * n)

    red[0].send_planes()

    transpose_into(tT, cs)
    put(mm(tT[...], dbs[...]), OUT_ROW)
    red[1].send_core()
    transpose_into(tT, h1s)

    def attention_back(p):
        sl = [slice(j * D + 128 * p, j * D + 128 * p + 128) for j in range(3)]

        @pl.loop(0, NI // 3)
        def _(c):
            rs = [pl.ds(pl.multiple_of((3 * c + m) * PAD, 16), PAD) for m in range(3)]
            q, k, v = ([qkv[r, t] for r in rs] for t in sl)
            dc = [dys[r, 128 * p:128 * p + 128] for r in rs]
            pr = [ps.at[(3 * c + m) * HEADS + 2 * p + h] for m in range(3) for h in range(2)]
            das = [mm_nt(dc[m // 2], half(v[m // 2], m % 2)) for m in range(6)]
            dss = []
            for m in range(6):
                prf = pr[m][...].astype(F32)
                t = prf * das[m]
                dss.append((t - prf * jnp.sum(t, axis=-1, keepdims=True)).astype(BF16))
            for m in range(3):
                a, b = 2 * m, 2 * m + 1
                dv = mm_tn(pr[a][...], half(dc[m], 0)) + mm_tn(pr[b][...], half(dc[m], 1))
                dq = mm(dss[a], half(k[m], 0)) + mm(dss[b], half(k[m], 1))
                dk = mm_tn(dss[a], half(q[m], 0)) + mm_tn(dss[b], half(q[m], 1))
                for j, o in enumerate((dq * 0.125, dk, dv)):
                    o = o.astype(BF16)
                    qkv[rs[m], sl[j]] = o
                    if j != 1:
                        gvec[6 + j:7 + j, 128 * p:128 * p + 128] += colsum(o.astype(F32))

    def qkv_grad(p):
        rhs = jnp.concatenate([qkv[:, j * D + 128 * p:j * D + 128 * p + 128] for j in range(3)], axis=1)
        put(mm(tT[...], rhs), QKV_ROW + 288 * p)

    attention_back(0)
    red[1].send_planes()
    qkv_grad(0)
    attention_back(1)
    red[0].send_row()
    qkv_grad(1)
    red[2].send_core()
    attention_back(2)
    red[0].send_back()
    red[2].send_planes()
    qkv_grad(2)
    red[3].send_core()
    red[1].send_row()
    out_copy.wait()

    def first_norm_back(a, b):
        @pl.loop(a // CH4, b // CH4)
        def _(c):
            r = pl.ds(pl.multiple_of(c * (CH4 * PAD), 16), CH4 * PAD)
            dh = mm_nt(qkv[r, :], wqkv[...])
            xs = jnp.concatenate([padded(x_ref, c * CH4 + j, tmp) for j in range(CH4)], axis=0)
            n1, rs1 = norm_parts(xs)
            gvec[0:1, :] += colsum(dh * n1)
            gvec[1:2, :] += colsum(dh)
            ig = dbs[r, :].astype(F32) + norm_back(dh * vec(0), n1, rs1)
            for j in range(CH4):
                stage[c * CH4 + j] = ig[j * PAD:j * PAD + SEQ].astype(BF16)

    first_norm_back(0, 4)
    red[3].send_planes()
    first_norm_back(4, 8)
    red[1].send_back()
    red[2].send_row()
    first_norm_back(8, 12)

    ig_copy = pltpu.make_async_copy(stage, ig_ref, out_sem)
    ig_copy.start()
    for b in range(4):
        gvec[9 + b:10 + b, :] = gub[0:1, b * D:b * D + D]
    gv = gvec[...]
    for s in range(4):
        moved = gv if s == 0 else pltpu.roll(gv, D - 96 * s, 1)
        bias = gv if s % 2 == 0 else pltpu.roll(gv, D - 192, 1)
        br = 6 if s < 2 else 8
        tile = jnp.concatenate(
            [moved[0:6, 0:128], bias[br:br + 1, 0:128], bias[br:br + 1, 128:256]]
            + [gv[9 + s:10 + s, 128 * b:128 * b + 128] for b in range(3)] + [jnp.zeros((5, 128), F32)],
            axis=0,
        )
        gradv[s % 2, s // 2] = tile.astype(BF16)
    redv.send_core()
    red[3].send_row()
    redv.send_planes()
    red[2].send_back()
    red[3].send_back()
    redv.send_row()
    for g in range(4):
        red[g].finish()
    redv.send_back()
    fin_copy = pltpu.make_async_copy(fin, fin_ref, x_sem)
    fin_copy.start()
    finv_ref[...] = finv[...]
    for j in range(5):
        first[j].wait_send()
        second[j].wait_send()
        third[j].wait_send()
    ig_copy.wait()
    fin_copy.wait()


def scratches():
    V = pltpu.VMEM
    bufs = []
    for n, full in ((64, 1024), (96, 1536), (32, 512), (32, 512), (16, 16)):
        bufs += [V((2, full, 128), BF16), V((15, 2, n, 128), BF16), V((2, n, 128), BF16), V((3, n, 128), BF16)]
    return [
        V((NI, SEQ, D), BF16), pltpu.SemaphoreType.DMA, V((NI, SEQ, D), BF16), pltpu.SemaphoreType.DMA,
        V((16, D), F32), V((16, D), BF16), V((PAD, D), F32), V((8, FF), F32), V((TROWS, D), BF16), V((D, TROWS), BF16), V((D, TROWS), BF16),
        V((TROWS, D), BF16), V((TROWS, 3 * D), BF16), V((NI * HEADS, PAD, PAD), BF16),
        V((TROWS, D), BF16), V((TROWS, D), BF16), V((TROWS, FF), BF16), V((TROWS, FF), BF16),
        V((TROWS, D), BF16),
        V((64, D), BF16), V((D, 3 * D), BF16), V((D, D), BF16), V((D, FF), BF16), V((FF, D), BF16),
        V((16, D), F32), V((16, D), F32), V((2, 2, GROWS, 128), BF16), V((2, 2, 16, 128), BF16),
        *bufs,
        V((GROWS, 128), BF16), V((16, 128), BF16),
        pltpu.SemaphoreType.DMA((200,)), pltpu.SemaphoreType.DMA((200,)),
    ]


def layer(x, dy, *params):
    S = jax.ShapeDtypeStruct
    vm, hbm = pl.BlockSpec(memory_space=pltpu.VMEM), pl.BlockSpec(memory_space=pl.ANY)
    return pl.pallas_call(
        body,
        out_shape=(S(x.shape, BF16), S(x.shape, BF16), S((GROWS, 128), BF16), S((16, 128), BF16)),
        in_specs=[hbm, hbm] + [vm] * 12, out_specs=(hbm, hbm, hbm, vm),
        scratch_shapes=scratches(),
        compiler_params=pltpu.CompilerParams(
            vmem_limit_bytes=int(63.5 * 2**20), collective_id=0, has_side_effects=True),
    )(x, dy, *params)


def unpack_body(out_in, ig_in, fin_in, finv, out, ig, g1, s1, gqkv, gqv, go, bo, g2, s2, gup, bup, gd, bd, fin, held, fin_sem, sems):
    fin_copy = pltpu.make_async_copy(fin_in, fin, fin_sem)
    fin_copy.start()
    pairs = ((out_in, out), (ig_in, ig))
    reads, copies = [], []
    for j, (src, dst) in enumerate(pairs):
        for p in range(4):
            some = pl.ds(3 * p, 3)
            reads.append(pltpu.make_async_copy(src.at[some], held.at[j, some], sems.at[0, 4 * j + p]))
            copies.append(pltpu.make_async_copy(held.at[j, some], dst.at[some], sems.at[1, 4 * j + p]))
    for read in reads:
        read.start()
    for read, copy in zip(reads, copies):
        read.wait()
        copy.start()
    fin_copy.wait()
    for b in range(12):
        gup[:, 128 * b:128 * b + 128] = fin[UP_ROW + 96 * b:UP_ROW + 96 * b + 96, :].astype(F32)
    for b in range(3):
        gd[128 * b:128 * b + 128, :] = fin[DOWN_ROW + 384 * b:DOWN_ROW + 384 * b + 384, :].astype(F32).T
        go[:, 128 * b:128 * b + 128] = fin[OUT_ROW + 96 * b:OUT_ROW + 96 * b + 96, :].astype(F32)
    for p in range(3):
        for j in range(3):
            r = QKV_ROW + 288 * p + 96 * j
            gqkv[:, j * D + 128 * p:j * D + 128 * p + 128] = fin[r:r + 96, :].astype(F32)
    v = finv[...].astype(F32)
    for row, ref in enumerate((g1, s1, bo, g2, s2, bd)):
        ref[...] = v[row, 0:96]
    gqv[0:128] = v[6, :]
    gqv[128:192] = v[7, 0:64]
    for b in range(3):
        bup[128 * b:128 * b + 128] = v[8 + b, :]
    for copy in copies:
        copy.wait()


def unpack(outputs, input_grad, fin, finv):
    def S(*shape):
        return jax.ShapeDtypeStruct(shape, F32)

    vm, hbm = pl.BlockSpec(memory_space=pltpu.VMEM), pl.BlockSpec(memory_space=pl.ANY)
    whole = jax.ShapeDtypeStruct(outputs.shape, BF16)
    return pl.pallas_call(
        unpack_body,
        out_shape=(whole, whole, S(96), S(96), S(96, 3 * D), S(192), S(96, D), S(96), S(96), S(96),
                   S(96, FF), S(384), S(384, D), S(96)),
        in_specs=[hbm, hbm, hbm, vm], out_specs=(hbm, hbm) + (vm,) * 12,
        scratch_shapes=[pltpu.VMEM(fin.shape, BF16), pltpu.VMEM((2, *outputs.shape), BF16), pltpu.SemaphoreType.DMA,
                        pltpu.SemaphoreType.DMA((2, 8))],
        compiler_params=pltpu.CompilerParams(vmem_limit_bytes=62 * 2**20),
    )(outputs, input_grad, fin, finv)


def local(*arrays):
    return unpack(*layer(*arrays))


def solution(mesh):
    tokens, whole, rows = P(("rep", "shard"), None, None), P("shard"), P("shard", None)
    vectors = (whole, whole, rows, whole, rows, whole, whole, whole, rows, whole, rows, whole)
    return jax.shard_map(
        local, mesh=mesh, in_specs=(tokens, tokens, *vectors),
        out_specs=(tokens, tokens, *vectors), check_vma=False)
```
